32 devices in a mesh: dp: 8 (over z, y), fsdp: 4 (over x, core).
Axes of the slice: x: 2, y: 2, z: 4, core: 2. Of those that a mesh axis runs over, the one named last changes fastest.
Arguments:
- tokens: bfloat16 [4096, 2048], P(('dp', 'fsdp')), may hold values from -6 to 6
- upstream: bfloat16 [4096, 512], P(('dp', 'fsdp')), may hold values from -6 to 6
- value_weight: bfloat16 [2048, 512], P('fsdp'), may hold values from -0.125 to 0.125
- forget_label: int32 [8], P('dp'), may hold values 0 or 1
- copy_index: int32 [8], P('dp'), may hold values from 0 to 1, as said below
- adv_rate: float32 [2], replicated, may hold values from 0.5 to 2
Outputs:
- meta_grad: float32 [2048, 512], P('fsdp')
The draws below stay inside these ranges and needn't reach their ends.
Inputs may be any that keep to these rules, and one draw needn't show every extreme that they name: `copy_index`: each of the 2 copies is named by exactly 4 sequences.
All inputs are finite; a program needn't handle non-finite values. No bound on the sum of `forget_label` on one device may be relied on, other than what follows from the above.
Results may differ from the reference program's by a relative error of at most 0.0056.
Values may be sent and summed in bfloat16 or wider, within the bound.
No kernel may reach another device: no remote copies, remote signals or barrier semaphores. Data moves between devices by JAX's collectives and lax.ppermute only.
A program may use at most 64 MiB of HBM per device.

```python
import math
import jax
import jax.numpy as jnp

DW = 2048
E = 512
COPIES = 2
LEN = 512
SEQS = 8
TOKENS = 4096


def draw_copy_index(key, part):
    order = jax.random.permutation(key, SEQS)
    return (order % COPIES).astype(jnp.int32)


def set_ends(entries, key, least, largest):
    longest = entries.shape.index(max(entries.shape))
    spots = []
    for shift in (0, 1):
        where = [jax.random.randint(jax.random.fold_in(key, axis), (), 0, length) for axis, length in enumerate(entries.shape)]
        where[longest] = (where[longest] + shift) % entries.shape[longest]
        spots.append(tuple(where))
    return entries.at[spots[0]].set(least).at[spots[1]].set(largest)


def shard_levels(own_key, dims, shards, least, high):
    gain = 1.0
    for position, parts in shards:
        draws = jax.random.uniform(jax.random.fold_in(jax.random.fold_in(own_key, 6), position), (parts,), jnp.float32, least / len(shards), high / len(shards))
        gain = gain * jnp.repeat(jnp.exp(draws), dims[position] // parts).reshape((-1,) + (1,) * (len(dims) - 1 - position))
    return gain


def bell_draw(key, shape, scale, bound, split=(), held_as=jnp.bfloat16):
    values = scale * jax.random.normal(key, shape, jnp.float32)
    if split:
        values = values * shard_levels(key, shape, split, -0.22, 0.18)
    return jnp.clip(values, -bound, bound).astype(held_as)


def setup_inputs(seed: int = 0) -> dict:
    keys = jax.random.split(jax.random.key(seed), 7)
    tokens = bell_draw(keys[0], (TOKENS, DW), 1.0, 6.0, ((0, 32),))
    upstream = bell_draw(keys[1], (TOKENS, E), 1.0, 6.0, ((0, 32),))
    value_weight = bell_draw(keys[2], (DW, E), DW ** -0.5, 0.125, ((0, 4),))
    forget_label = set_ends((jax.random.randint(keys[3], (SEQS,), 0, 2) < 1).astype(jnp.int32), jax.random.fold_in(keys[3], 1), 0, 1)
    copy_index = draw_copy_index(jax.random.fold_in(keys[6], 71), 0)
    adv_rate = jnp.clip(jnp.exp(jax.random.uniform(keys[5], (COPIES,), jnp.float32, math.log(0.5), math.log(2.0))), 0.5, 2.0)
    return dict(tokens=tokens, upstream=upstream, value_weight=value_weight, forget_label=forget_label, copy_index=copy_index, adv_rate=adv_rate)


def first_slope(value):
    sig = jax.nn.sigmoid(value)
    return sig * (1.0 + value * (1.0 - sig))


def second_slope(value):
    sig = jax.nn.sigmoid(value)
    return sig * (1.0 - sig) * (2.0 + value * (1.0 - 2.0 * sig))


def reference(tokens, upstream, value_weight, forget_label, copy_index, adv_rate):
    inputs = tokens.reshape(SEQS, LEN, DW).astype(jnp.float32)
    upward = upstream.reshape(SEQS, LEN, E).astype(jnp.float32)
    forget = forget_label.astype(jnp.float32)[:, None, None]
    onehot = (copy_index[:, None] == jnp.arange(COPIES, dtype=jnp.int32)[None, :]).astype(jnp.float32)
    weight_f = value_weight.astype(jnp.float32)
    primal = jnp.einsum("std,de->ste", inputs, weight_f)
    delta_adv = (forget * upward * first_slope(primal) / LEN).astype(jnp.bfloat16)
    per_seq = jnp.einsum("std,ste->sde", inputs, delta_adv.astype(jnp.float32))
    grad_copy = jnp.einsum("sc,sde->cde", onehot, per_seq)
    attacked = (weight_f[None] - adv_rate[:, None, None] * grad_copy).astype(jnp.bfloat16)
    attacked_seq = jnp.einsum("sc,cde->sde", onehot, attacked.astype(jnp.float32))
    altered = jnp.einsum("std,sde->ste", inputs, attacked_seq)
    delta_out = ((1.0 - 2.0 * forget) * upward * first_slope(altered) / LEN).astype(jnp.bfloat16)
    outer_seq = jnp.einsum("std,ste->sde", inputs, delta_out.astype(jnp.float32))
    outer_copy = jnp.einsum("sc,sde->cde", onehot, outer_seq)
    tangent = outer_copy.astype(jnp.bfloat16)
    tangent_seq = jnp.einsum("sc,cde->sde", onehot, tangent.astype(jnp.float32))
    forward_tangent = jnp.einsum("std,sde->ste", inputs, tangent_seq)
    delta_curv = (forget * upward * second_slope(primal) * forward_tangent / LEN).astype(jnp.bfloat16)
    curv_seq = jnp.einsum("std,ste->sde", inputs, delta_curv.astype(jnp.float32))
    rate_seq = jnp.sum(onehot * adv_rate[None, :], axis=1)
    curv_sum = jnp.einsum("s,sde->de", rate_seq, curv_seq)
    scale = (float(LEN) / float(SEQS)) ** 0.5
    return scale * (jnp.sum(outer_copy, axis=0) - curv_sum)
```

```python
import jax
import jax.numpy as jnp
from jax import lax
from jax.sharding import PartitionSpec as P

BF = jnp.bfloat16
F32 = jnp.float32


def first_slope(value):
    sig = jax.nn.sigmoid(value)
    return sig * (1.0 + value * (1.0 - sig))


def second_slope(value):
    sig = jax.nn.sigmoid(value)
    return sig * (1.0 - sig) * (2.0 + value * (1.0 - 2.0 * sig))


def swap(value, axis, bit):
    return lax.ppermute(value, axis, [(i, i ^ bit) for i in range(lax.axis_size(axis))])


def bits_of(size):
    found = []
    bit = 1
    while bit < size:
        found.append(bit)
        bit *= 2
    return found


def pick(value, axis, index, size):
    return lax.dynamic_slice_in_dim(value, index * size, size, axis)


def in_order(mine, other, upper, axis):
    return jnp.where(
        upper == 1,
        jnp.concatenate([other, mine], axis),
        jnp.concatenate([mine, other], axis),
    )


def over_tokens(left, tokens):
    return lax.dot_general(left, tokens, (((1,), (1,)), ((), ())), preferred_element_type=F32)


def over_rows(left, tokens):
    return jnp.dot(left, tokens, preferred_element_type=F32)


def local(tokens, upstream, value_weight, forget_label, copy_index, adv_rate):
    dp, fsdp = lax.axis_size("dp"), lax.axis_size("fsdp")
    rows, features = tokens.shape
    outs = upstream.shape[1]
    wide = outs // dp
    part = features // fsdp
    copies = adv_rate.shape[0]
    seq_length = rows * fsdp
    me = lax.axis_index("dp")
    quarter = lax.axis_index("fsdp")
    core = quarter % 2
    dp_bits = bits_of(dp)[::-1]
    far_bits = bits_of(fsdp)[1:]

    blocks = {0: tokens}
    for r in range(1, dp):
        bit = r & -r
        blocks[r] = swap(blocks[r ^ bit], "dp", bit)

    weight = pick(value_weight, 1, me, wide).T
    for bit in bits_of(fsdp):
        weight = in_order(weight, swap(weight, "fsdp", bit), (quarter // bit) % 2, 1)

    up = upstream.T
    labels = jnp.stack([forget_label[0], copy_index[0]] + [jnp.int32(0)] * 14).astype(BF)
    labels = jnp.broadcast_to(labels[:, None], (16, rows))
    order = [0]
    for bit in dp_bits:
        half = up.shape[0] // 2
        side = (me // bit) % 2
        sent = jnp.concatenate([pick(up, 0, 1 - side, half), labels])
        came = swap(sent, "dp", bit)
        up = jnp.concatenate([pick(up, 0, side, half), came[:half]], 1)
        labels = jnp.concatenate([labels, came[half:]], 1)
        order = order + [r ^ bit for r in order]
    up = up.astype(F32)
    forget = labels[0:1].astype(F32)
    copy = labels[1:2].astype(F32)
    held = jnp.concatenate([blocks[r] for r in order])

    onehot = [(copy == float(c)).astype(F32) for c in range(copies)]
    own_rate = sum(onehot[c] * adv_rate[c] for c in range(copies))

    def by_copy(value):
        return jnp.concatenate([(value * onehot[c]) for c in range(copies)]).astype(BF)

    def of_copy(value):
        value = value.reshape(copies, wide, -1)
        return sum(value[c] * onehot[c] for c in range(copies))

    def core_half(value, side):
        m = value.shape[0]
        value = value.reshape(m, fsdp // 2, 2, part)
        return lax.dynamic_index_in_dim(value, side, 2, False).reshape(m, features // 2)

    def both_halves(mine, other):
        m = mine.shape[0]
        mine = mine.reshape(m, fsdp // 2, 1, part)
        other = other.reshape(m, fsdp // 2, 1, part)
        return in_order(mine, other, core, 2).reshape(m, features)

    def total(value):
        came = swap(core_half(value, 1 - core).astype(BF), "fsdp", 1)
        value = core_half(value, core) + came.astype(F32)
        for bit in far_bits:
            value = value + swap(value.astype(BF), "fsdp", bit).astype(F32)
        return value

    primal = over_tokens(weight, held)
    delta_adv = (forget * up * first_slope(primal) / seq_length).astype(BF)
    grad = total(over_rows(by_copy(delta_adv.astype(F32)), held))
    rates = jnp.repeat(adv_rate, wide)[:, None]
    half_weight = jnp.concatenate([core_half(weight, core)] * copies).astype(F32)
    attacked = (half_weight - rates * grad).astype(BF)
    attacked = both_halves(attacked, swap(attacked, "fsdp", 1))
    altered = of_copy(over_tokens(attacked, held))
    delta_out = ((1.0 - 2.0 * forget) * up * first_slope(altered) / seq_length).astype(BF)
    outer = total(over_rows(by_copy(delta_out.astype(F32)), held))
    tangent = outer.astype(BF)
    tangent = both_halves(tangent, swap(tangent, "fsdp", 1))
    forward_tangent = of_copy(over_tokens(tangent, held))
    delta_curv = (forget * up * second_slope(primal) * forward_tangent / seq_length).astype(BF)
    curv = over_rows((own_rate * delta_curv.astype(F32)).astype(BF), held)

    came = swap(core_half(curv, 1 - core).astype(BF), "fsdp", 1)
    curv = core_half(curv, core) + came.astype(F32)
    for bit in far_bits[::-1]:
        half = curv.shape[1] // 2
        side = (quarter // bit) % 2
        came = swap(pick(curv, 1, 1 - side, half).astype(BF), "fsdp", bit)
        curv = pick(curv, 1, side, half) + came.astype(F32)
    outer = outer.reshape(copies, wide, features // 2).sum(0)
    outer = pick(outer, 1, quarter // 2, part)
    scale = (float(seq_length) / float(dp)) ** 0.5
    result = (scale * (outer - curv)).astype(BF)
    for bit in dp_bits:
        result = jnp.stack([result, swap(result, "dp", bit)])
        result = result.reshape(-1, part)
    result = result.reshape([2] * len(dp_bits) + [wide, part])
    for place, bit in enumerate(dp_bits[::-1]):
        side = (me // bit) % 2
        result = jnp.where(side == 1, jnp.flip(result, place), result)
    axes = tuple(range(len(dp_bits)))
    result = result.transpose(axes[::-1] + (len(axes), len(axes) + 1))
    return result.reshape(outs, part).T.astype(F32)


def solution(mesh):
    in_specs = (
        P(("dp", "fsdp"), None),
        P(("dp", "fsdp"), None),
        P("fsdp", None),
        P("dp"),
        P("dp"),
        P(),
    )
    out_specs = P("fsdp", None)
    return jax.shard_map(local, mesh=mesh, in_specs=in_specs, out_specs=out_specs, check_vma=False)
```

```python
import functools

import jax
import jax.numpy as jnp
from jax import lax
from jax.experimental import pallas as pl
from jax.experimental.pallas import tpu as pltpu
from jax.sharding import PartitionSpec as P

BF = jnp.bfloat16
F32 = jnp.float32


def first_slope(value):
    sig = jax.nn.sigmoid(value)
    return sig * (1.0 + value * (1.0 - sig))


def second_slope(value):
    sig = jax.nn.sigmoid(value)
    return sig * (1.0 - sig) * (2.0 + value * (1.0 - 2.0 * sig))


def swap(value, axis, bit):
    return lax.ppermute(value, axis, [(i, i ^ bit) for i in range(lax.axis_size(axis))])


def after(value, *others):
    return lax.optimization_barrier((value,) + others)[0]


def bits_of(size):
    found = []
    bit = 1
    while bit < size:
        found.append(bit)
        bit *= 2
    return found


def onehots(labels, copies):
    copy = labels[1:2, :].astype(F32)
    return [(copy == float(c)).astype(F32) for c in range(copies)]


def over_tiles(count, body):
    if count == 1:
        body(0)
    else:
        lax.fori_loop(0, count, lambda tile, none: body(tile), None)


def tile_at(tile, size):
    return pl.ds(tile * size if isinstance(tile, int) else pl.multiple_of(tile * size, size), size)


def times_tokens(core, part, pairs, mine, other, held, rows):
    total = None
    for j in range(pairs):
        for value, side in ((mine, core), (other, 1 - core)):
            columns = pl.ds(pl.multiple_of((2 * j + side) * part, part), part)
            term = lax.dot_general(
                value[:, pl.ds(j * part, part)],
                held[rows, columns],
                (((1,), (1,)), ((), ())),
                preferred_element_type=F32,
            )
            total = term if total is None else total + term
    return total


def contract(core, part, pairs, delta, held, rows, send, keep, sums):
    only = rows.size == held.shape[0]
    for j in range(pairs):
        place = pl.ds(j * part, part)
        for out, side in ((send if only else sums, 1 - core), (keep, core)):
            columns = pl.ds(pl.multiple_of((2 * j + side) * part, part), part)
            term = jnp.dot(delta, held[rows, columns], preferred_element_type=F32)
            out[:, place] = (term if only else out[:, place] + term).astype(out.dtype)


def each_tile(held, send, keep, sums, body):
    size = min(held.shape[0], 1024)
    count = held.shape[0] // size
    if count > 1:
        keep[...] = jnp.zeros_like(keep)
        sums[...] = jnp.zeros_like(sums)
    over_tiles(count, lambda tile: body(tile_at(tile, size)))
    if count > 1:
        send[...] = sums[...].astype(BF)


def of_copy(value, hots):
    wide = value.shape[0] // len(hots)
    return sum(value[c * wide : (c + 1) * wide] * hot for c, hot in enumerate(hots))


def by_copy(delta, hots):
    delta = delta.astype(F32)
    return jnp.concatenate([delta * hot for hot in hots], 0).astype(BF)


def prepare_kernel(wide, side_of, scalars, upstream, value_weight, weight, up, labels, sent, turned):
    me = scalars[0]
    group = 128 // wide
    columns = pl.ds(pl.multiple_of((me // group) * 128, 128), 128)
    turned[...] = value_weight[:, columns].astype(F32).T
    own = pl.ds(pl.multiple_of((me % group) * wide, wide), wide)
    weight[...] = turned[own, :].astype(BF)
    up[...] = upstream[...].astype(F32).T.astype(BF)
    row = lax.broadcasted_iota(jnp.int32, labels.shape, 0)
    both = jnp.where(row == 0, scalars[2], jnp.where(row == 1, scalars[3], 0))
    labels[...] = both.astype(F32).astype(BF)
    every_second(up, 1 - side_of(me), wide, sent)
    sent[pl.ds(up.shape[0] // 2, 16), :] = labels[...]


def every_second(source, side, wide, target, columns=slice(None)):
    for k in range(source.shape[0] // wide // 2):
        block = pl.ds(pl.multiple_of((2 * k + side) * wide, wide), wide)
        target[pl.ds(k * wide, wide), columns] = source[block, :]


def join_kernel(wide, side_of, next_side, scalars, up, labels, came, new_up, new_labels, *sent):
    me = scalars[0]
    half, long = up.shape[0] // 2, up.shape[1]
    every_second(up, side_of(me), wide, new_up, pl.ds(0, long))
    new_up[:, pl.ds(long, long)] = came[pl.ds(0, half), :]
    new_labels[:, pl.ds(0, long)] = labels[...]
    new_labels[:, pl.ds(long, long)] = came[pl.ds(half, 16), :]
    if sent:
        every_second(new_up, 1 - next_side(me), wide, sent[0])
        sent[0][pl.ds(half // 2, 16), :] = new_labels[...]


def first_kernel(sizes, scalars, *refs):
    part, pairs, copies, length, count = sizes
    pieces, (weight, up, labels, held, primal_out, send, keep, sums) = refs[:count], refs[count:]
    quarter = scalars[1]
    row = 0
    for piece in pieces:
        held[pl.ds(row, piece.shape[0]), :] = piece[...]
        row += piece.shape[0]
    wide = up.shape[0]

    def body(rows):
        primal = None
        for i in range(2 * pairs):
            columns = pl.ds(pl.multiple_of((quarter ^ i) * part, part), part)
            term = lax.dot_general(
                weight[pl.ds(i * wide, wide), :],
                held[rows, columns],
                (((1,), (1,)), ((), ())),
                preferred_element_type=F32,
            )
            primal = term if primal is None else primal + term
        primal_out[:, rows] = primal
        hots = onehots(labels[:, rows], copies)
        forget = labels[0:1, rows].astype(F32)
        delta = (forget * up[:, rows].astype(F32) * first_slope(primal) / length).astype(BF)
        contract(quarter % 2, part, pairs, by_copy(delta, hots), held, rows, send, keep, sums)

    each_tile(held, send, keep, sums, body)


def second_kernel(sizes, scalars, held, mine, other, up, labels, send, keep, sums):
    part, pairs, copies, length = sizes
    core = scalars[1] % 2

    def body(rows):
        hots = onehots(labels[:, rows], copies)
        altered = of_copy(times_tokens(core, part, pairs, mine, other, held, rows), hots)
        sign = 1.0 - 2.0 * labels[0:1, rows].astype(F32)
        delta = (sign * up[:, rows].astype(F32) * first_slope(altered) / length).astype(BF)
        contract(core, part, pairs, by_copy(delta, hots), held, rows, send, keep, sums)

    each_tile(held, send, keep, sums, body)


def third_kernel(sizes, scalars, rate, held, mine, other, up, labels, primal, send, keep, sums):
    part, pairs, copies, length = sizes
    core = scalars[1] % 2

    def body(rows):
        hots = onehots(labels[:, rows], copies)
        forward = of_copy(times_tokens(core, part, pairs, mine, other, held, rows), hots)
        forget = labels[0:1, rows].astype(F32)
        own_rate = sum(hot * rate[c] for c, hot in enumerate(hots))
        slope = second_slope(primal[:, rows])
        delta = (forget * up[:, rows].astype(F32) * slope * forward / length).astype(BF)
        delta = (own_rate * delta.astype(F32)).astype(BF)
        contract(core, part, pairs, delta, held, rows, send, keep, sums)

    each_tile(held, send, keep, sums, body)


def add_kernel(mine, came, total, sent):
    value = mine[...] + came[...].astype(F32)
    total[...] = value
    sent[...] = value.astype(BF)


def attack_kernel(copies, scalars, rate, mine, came, weight, attacked):
    quarter = scalars[1]
    part = weight.shape[1]
    wide = mine.shape[0] // copies
    for j in range(mine.shape[1] // part):
        place = quarter ^ (2 * j + quarter % 2)
        own = weight[pl.ds(pl.multiple_of(place * wide, wide), wide), :].astype(F32)
        columns = pl.ds(j * part, part)
        for c in range(copies):
            rows = pl.ds(c * wide, wide)
            grad = mine[rows, columns] + came[rows, columns].astype(F32)
            attacked[rows, columns] = (own - rate[c] * grad).astype(BF)


def tangent_kernel(copies, scalars, mine, came, tangent, outer):
    value = mine[...] + came[...].astype(F32)
    tangent[...] = value.astype(BF)
    wide, part = outer.shape
    own = pl.ds(pl.multiple_of((scalars[1] // 2) * part, part), part)
    outer[...] = sum(
        mine[pl.ds(c * wide, wide), own] + came[pl.ds(c * wide, wide), own].astype(F32)
        for c in range(copies)
    )


def halve_kernel(bit, scalars, mine, came, total, sent, whole):
    whole[...] = mine[...] + came[...].astype(F32)
    half = total.shape[1]
    side = (scalars[1] // bit) % 2
    total[...] = whole[:, pl.ds(pl.multiple_of(side * half, half), half)]
    sent[...] = whole[:, pl.ds(pl.multiple_of((1 - side) * half, half), half)].astype(BF)


def result_kernel(scale, outer, mine, came, result):
    result[...] = (scale * (outer[...] - (mine[...] + came[...].astype(F32)))).astype(BF)


def place_kernel(order, scalars, *refs):
    blocks, out = refs[:-1], refs[-1]
    me = scalars[0]
    wide = blocks[0].shape[0]
    flat = []
    for ref in blocks:
        flat += [ref[pl.ds(row, wide), :].astype(F32) for row in range(0, ref.shape[0], wide)]
    where = {r: flat[i] for i, r in enumerate(order)}
    for r in order:
        if r % 2:
            continue
        low, high = where[r], where[r ^ 1]
        odd = me % 2 == 1
        pair = jnp.concatenate([jnp.where(odd, high, low), jnp.where(odd, low, high)], 0)
        columns = pl.ds(pl.multiple_of(((me ^ r) // 2) * 128, 128), 128)
        out[:, columns] = pair.T


def run(kernel, scalars, arrays, outs, scratch=()):
    nbytes = sum(a.size * a.dtype.itemsize for a in arrays)
    nbytes += sum(s[0] * s[1] * jnp.dtype(t).itemsize for s, t in outs)
    smem = pl.BlockSpec(memory_space=pltpu.SMEM)
    vmem = pl.BlockSpec(memory_space=pltpu.VMEM)
    return pl.pallas_call(
        kernel,
        out_shape=[jax.ShapeDtypeStruct(s, t) for s, t in outs],
        in_specs=[smem] * len(scalars) + [vmem] * len(arrays),
        out_specs=[vmem] * len(outs),
        scratch_shapes=[pltpu.VMEM(s, t) for s, t in scratch],
        compiler_params=pltpu.CompilerParams(vmem_limit_bytes=nbytes + (8 << 20)),
    )(*scalars, *arrays)


def local(tokens, upstream, value_weight, forget_label, copy_index, adv_rate):
    dp, fsdp = lax.axis_size("dp"), lax.axis_size("fsdp")
    rows, features = tokens.shape
    outs = upstream.shape[1]
    wide = outs // dp
    part = features // fsdp
    pairs = fsdp // 2
    copies = adv_rate.shape[0]
    seq_length = rows * fsdp
    held_rows = rows * dp
    me = lax.axis_index("dp").astype(jnp.int32)
    quarter = lax.axis_index("fsdp").astype(jnp.int32)
    scalars = jnp.stack([me, quarter, forget_label[0], copy_index[0]])
    dp_bits = bits_of(dp)[::-1]
    far_bits = bits_of(fsdp)[1:]
    up_bits = dp_bits[::-1]

    def side_of(bit):
        return lambda me: (me // bit) % 2

    weight, up, labels, sent = run(
        functools.partial(prepare_kernel, wide, side_of(up_bits[0])),
        [scalars],
        [upstream, value_weight],
        [((wide, part), BF), ((outs, rows), BF), ((16, rows), BF), ((outs // 2 + 16, rows), BF)],
        [((128, part), F32)],
    )

    top_bit = dp_bits[0]
    tops = [top_bit]
    for bit in dp_bits[1:]:
        tops.append(tops[-1] | bit)
    half_rows = rows // 2
    first = {0: tokens[:half_rows]}
    second = {0: tokens[half_rows:]}
    whole = {0: tokens}
    late = {}
    for step, (top, up_bit) in enumerate(zip(tops, up_bits), 1):
        wholes, firsts = {}, {}
        new_late = {}
        for r in range(1, dp):
            if bin(r).count("1") != step:
                continue
            bit = r & -r
            if r < top_bit:
                wholes[r] = swap(whole[r ^ bit], "dp", bit)
                continue
            way = 2 * bit if r == dp - 1 and dp > 2 else bit
            firsts[r] = swap(first[r ^ way], "dp", way)
            if r != top:
                new_late[r] = swap({**second, **late}[r ^ bit], "dp", bit)
        came_up = swap(sent, "dp", up_bit)
        wholes, came_up = lax.optimization_barrier((wholes, came_up))
        firsts, late = lax.optimization_barrier((firsts, late))
        whole.update(wholes)
        first.update(firsts)
        second.update(late)
        late = new_late
        second[top] = swap(second[top ^ dp_bits[step - 1]], "dp", dp_bits[step - 1])
        high, long = up.shape[0] // 2, 2 * up.shape[1]
        shapes = [((high, long), BF), ((16, long), BF)]
        if step < len(dp_bits):
            shapes.append(((high // 2 + 16, long), BF))
        following = side_of(up_bits[step]) if step < len(dp_bits) else None
        joined = run(
            functools.partial(join_kernel, wide, side_of(up_bit), following),
            [scalars],
            [up, labels, came_up],
            shapes,
        )
        up, labels = joined[:2]
        sent = joined[-1]
    second.update(late)
    order = [0]
    for bit in up_bits:
        order = order + [r ^ bit for r in order]
    flat = []
    for r in order:
        flat += [whole[r]] if r in whole else [first[r], second[r]]

    weight = after(weight, first[top_bit])
    for bit in bits_of(fsdp):
        weight = jnp.concatenate([weight, swap(weight, "fsdp", bit)])

    def total(send, keep, bits):
        shape = keep.shape
        came = swap(send, "fsdp", 1)
        for bit in bits:
            keep, sent = run(add_kernel, [], [keep, came], [(shape, F32), (shape, BF)])
            came = swap(sent, "fsdp", bit)
        return keep, came

    sizes = (part, pairs, copies, seq_length)
    stacked = (copies * wide, features // 2)
    held, primal, send, keep = run(
        functools.partial(first_kernel, sizes + (len(flat),)),
        [scalars],
        flat + [weight, up, labels],
        [((held_rows, features), BF), ((wide, held_rows), F32), (stacked, BF), (stacked, F32)],
        [(stacked, F32)],
    )
    (attacked,) = run(
        functools.partial(attack_kernel, copies),
        [scalars, adv_rate],
        [*total(send, keep, far_bits), weight],
        [(stacked, BF)],
    )
    send, keep = run(
        functools.partial(second_kernel, sizes),
        [scalars],
        [held, attacked, swap(attacked, "fsdp", 1), up, labels],
        [(stacked, BF), (stacked, F32)],
        [(stacked, F32)],
    )
    tangent, outer = run(
        functools.partial(tangent_kernel, copies),
        [scalars],
        [*total(send, keep, far_bits)],
        [(stacked, BF), ((wide, part), F32)],
    )
    send, keep = run(
        functools.partial(third_kernel, sizes),
        [scalars, adv_rate],
        [held, tangent, swap(tangent, "fsdp", 1), up, labels, primal],
        [((wide, features // 2), BF), ((wide, features // 2), F32)],
        [((wide, features // 2), F32)],
    )

    came = swap(send, "fsdp", 1)
    for bit in far_bits[::-1]:
        shape = (wide, keep.shape[1] // 2)
        keep, sent = run(
            functools.partial(halve_kernel, bit),
            [scalars],
            [keep, came],
            [(shape, F32), (shape, BF)],
            [(keep.shape, F32)],
        )
        came = swap(sent, "fsdp", bit)
    scale = (float(seq_length) / float(dp)) ** 0.5
    (result,) = run(
        functools.partial(result_kernel, scale), [], [outer, keep, came], [((wide, part), BF)]
    )
    blocks = [result]
    came_order = [0]
    for bit in dp_bits:
        came_order = came_order + [r ^ bit for r in came_order]
        sent = blocks[0] if len(blocks) == 1 else jnp.concatenate(blocks)
        blocks.append(swap(sent, "dp", bit))
    if 2 * wide == 128:
        (placed,) = run(
            functools.partial(place_kernel, came_order), [scalars], blocks, [((part, outs), F32)]
        )
        return placed
    result = jnp.concatenate(blocks).reshape([2] * len(dp_bits) + [wide, part])
    for place, bit in enumerate(dp_bits[::-1]):
        side = (me // bit) % 2
        result = jnp.where(side == 1, jnp.flip(result, place), result)
    axes = tuple(range(len(dp_bits)))
    result = result.transpose(axes[::-1] + (len(axes), len(axes) + 1))
    return result.reshape(outs, part).T.astype(F32)


def solution(mesh):
    in_specs = (
        P(("dp", "fsdp"), None),
        P(("dp", "fsdp"), None),
        P("fsdp", None),
        P("dp"),
        P("dp"),
        P(),
    )
    out_specs = P("fsdp", None)
    return jax.shard_map(local, mesh=mesh, in_specs=in_specs, out_specs=out_specs, check_vma=False)
```

```python
import functools

import jax
import jax.numpy as jnp
from jax import lax
from jax.experimental import pallas as pl
from jax.experimental.pallas import tpu as pltpu
from jax.sharding import PartitionSpec as P

BF = jnp.bfloat16
F32 = jnp.float32


def first_slope(value):
    sig = jax.nn.sigmoid(value)
    return sig * (1.0 + value * (1.0 - sig))


def second_slope(value):
    sig = jax.nn.sigmoid(value)
    return sig * (1.0 - sig) * (2.0 + value * (1.0 - 2.0 * sig))


def swap(value, axis, bit):
    return lax.ppermute(value, axis, [(i, i ^ bit) for i in range(lax.axis_size(axis))])


def after(value, *others):
    return lax.optimization_barrier((value,) + others)[0]


def bits_of(size):
    found = []
    bit = 1
    while bit < size:
        found.append(bit)
        bit *= 2
    return found


def onehots(labels, copies):
    copy = labels[1:2, :].astype(F32)
    return [(copy == float(c)).astype(F32) for c in range(copies)]


def times_tokens(core, part, pairs, mine, other, held, rows):
    total = None
    for j in range(pairs):
        for value, side in ((mine, core), (other, 1 - core)):
            columns = pl.ds(pl.multiple_of((2 * j + side) * part, part), part)
            term = lax.dot_general(
                value[:, pl.ds(j * part, part)],
                held[rows, columns],
                (((1,), (1,)), ((), ())),
                preferred_element_type=F32,
            )
            total = term if total is None else total + term
    return total


def contract(core, part, pairs, delta, held, rows, send, keep, before):
    for j in range(pairs):
        place = pl.ds(j * part, part)
        for k, (out, side) in enumerate(((send, 1 - core), (keep, core))):
            columns = pl.ds(pl.multiple_of((2 * j + side) * part, part), part)
            term = jnp.dot(delta, held[rows, columns], preferred_element_type=F32)
            if before is not None:
                term = before[k][:, place] + term
            out[:, place] = term.astype(out.dtype)


def in_tiles(held, sums, keep, body):
    tile = min(held.shape[0], 1024)
    if held.shape[0] == tile:
        body(pl.ds(0, tile), None)
        return
    sums[...] = jnp.zeros_like(sums)
    keep[...] = jnp.zeros_like(keep)

    def step(i, none):
        body(pl.ds(pl.multiple_of(i * tile, tile), tile), (sums, keep))

    lax.fori_loop(0, held.shape[0] // tile, step, None)


def of_copy(value, hots):
    wide = value.shape[0] // len(hots)
    return sum(value[c * wide : (c + 1) * wide] * hot for c, hot in enumerate(hots))


def by_copy(delta, hots):
    delta = delta.astype(F32)
    return jnp.concatenate([delta * hot for hot in hots], 0).astype(BF)


def prepare_kernel(wide, side_of, stride, scalars, upstream, value_weight, weight, up, labels, sent, turned):
    me = scalars[0]
    group = 128 // wide
    columns = pl.ds(pl.multiple_of((me // group) * 128, 128), 128)
    turned[...] = value_weight[:, columns].astype(F32).T
    own = pl.ds(pl.multiple_of((me % group) * wide, wide), wide)
    weight[...] = turned[own, :].astype(BF)
    up[...] = upstream[...].astype(F32).T.astype(BF)
    row = lax.broadcasted_iota(jnp.int32, labels.shape, 0)
    both = jnp.where(row == 0, scalars[2], jnp.where(row == 1, scalars[3], 0))
    labels[...] = both.astype(F32).astype(BF)
    every_second(up, 1 - side_of(me), stride, wide, sent)
    sent[pl.ds(up.shape[0] // 2, 16), :] = labels[...]


def every_second(source, side, stride, wide, target, columns=slice(None)):
    for k in range(source.shape[0] // wide // 2):
        place = (2 * (k // stride) + side) * stride + k % stride
        block = pl.ds(pl.multiple_of(place * wide, wide), wide)
        target[pl.ds(k * wide, wide), columns] = source[block, :]


def join_kernel(wide, side_of, stride, next_side, next_stride, scalars, up, labels, came, new_up, new_labels, *sent):
    me = scalars[0]
    half, long = up.shape[0] // 2, up.shape[1]
    every_second(up, side_of(me), stride, wide, new_up, pl.ds(0, long))
    new_up[:, pl.ds(long, long)] = came[pl.ds(0, half), :]
    new_labels[:, pl.ds(0, long)] = labels[...]
    new_labels[:, pl.ds(long, long)] = came[pl.ds(half, 16), :]
    if sent:
        every_second(new_up, 1 - next_side(me), next_stride, wide, sent[0])
        sent[0][pl.ds(half // 2, 16), :] = new_labels[...]


def first_kernel(sizes, places, last, scalars, *refs):
    part, pairs, copies, length = sizes
    refs, outs = refs[:-6], refs[-6:]
    before, refs = (refs[-2:], refs[:-2]) if last else (None, refs)
    pieces, (all_up, all_labels, weight) = refs[:-3], refs[-3:]
    held, up, labels, primal_out, sums, keep = outs
    quarter = scalars[1]
    wide = up.shape[0]
    row = 0
    for piece in pieces:
        held[pl.ds(row, piece.shape[0]), :] = piece[...]
        row += piece.shape[0]
    rows = held.shape[0] // len(places)
    for i, place in enumerate(places):
        up[:, pl.ds(i * rows, rows)] = all_up[:, pl.ds(place * rows, rows)]
        labels[:, pl.ds(i * rows, rows)] = all_labels[:, pl.ds(place * rows, rows)]

    def body(rows, prior):
        primal = None
        for i in range(2 * pairs):
            columns = pl.ds(pl.multiple_of((quarter ^ i) * part, part), part)
            term = lax.dot_general(
                weight[pl.ds(i * wide, wide), :],
                held[rows, columns],
                (((1,), (1,)), ((), ())),
                preferred_element_type=F32,
            )
            primal = term if primal is None else primal + term
        primal_out[:, rows] = primal
        hots = onehots(labels[:, rows], copies)
        forget = labels[0:1, rows].astype(F32)
        delta = (forget * up[:, rows].astype(F32) * first_slope(primal) / length).astype(BF)
        contract(quarter % 2, part, pairs, by_copy(delta, hots), held, rows, sums, keep, prior)

    if last:
        body(pl.ds(0, held.shape[0]), before)
    else:
        in_tiles(held, sums, keep, body)


def in_parts(parts, send, keep, sums, body):
    early, late = parts
    in_tiles(
        early[0], sums, keep, lambda rows, before: body(early, rows, sums, keep, before)
    )
    body(late, pl.ds(0, late[0].shape[0]), send, keep, (sums, keep))


def second_kernel(sizes, scalars, *refs):
    part, pairs, copies, length = sizes
    early, late, (mine, other, send, keep, sums) = refs[:3], refs[3:6], refs[6:]
    core = scalars[1] % 2

    def body(tokens, rows, send, keep, before):
        held, up, labels = tokens
        hots = onehots(labels[:, rows], copies)
        altered = of_copy(times_tokens(core, part, pairs, mine, other, held, rows), hots)
        sign = 1.0 - 2.0 * labels[0:1, rows].astype(F32)
        delta = (sign * up[:, rows].astype(F32) * first_slope(altered) / length).astype(BF)
        contract(core, part, pairs, by_copy(delta, hots), held, rows, send, keep, before)

    in_parts((early, late), send, keep, sums, body)


def third_kernel(sizes, scalars, rate, *refs):
    part, pairs, copies, length = sizes
    early, late, (mine, other, send, keep, sums) = refs[:4], refs[4:8], refs[8:]
    core = scalars[1] % 2

    def body(tokens, rows, send, keep, before):
        held, up, labels, primal = tokens
        hots = onehots(labels[:, rows], copies)
        forward = of_copy(times_tokens(core, part, pairs, mine, other, held, rows), hots)
        forget = labels[0:1, rows].astype(F32)
        own_rate = sum(hot * rate[c] for c, hot in enumerate(hots))
        slope = second_slope(primal[:, rows])
        delta = (forget * up[:, rows].astype(F32) * slope * forward / length).astype(BF)
        delta = (own_rate * delta.astype(F32)).astype(BF)
        contract(core, part, pairs, delta, held, rows, send, keep, before)

    in_parts((early, late), send, keep, sums, body)


def add_kernel(mine, came, total, sent):
    value = mine[...] + came[...].astype(F32)
    total[...] = value
    sent[...] = value.astype(BF)


def attack_kernel(copies, scalars, rate, mine, came, weight, attacked):
    quarter = scalars[1]
    part = weight.shape[1]
    wide = mine.shape[0] // copies
    for j in range(mine.shape[1] // part):
        place = quarter ^ (2 * j + quarter % 2)
        own = weight[pl.ds(pl.multiple_of(place * wide, wide), wide), :].astype(F32)
        columns = pl.ds(j * part, part)
        for c in range(copies):
            rows = pl.ds(c * wide, wide)
            grad = mine[rows, columns] + came[rows, columns].astype(F32)
            attacked[rows, columns] = (own - rate[c] * grad).astype(BF)


def tangent_kernel(copies, scalars, mine, came, tangent, outer):
    value = mine[...] + came[...].astype(F32)
    tangent[...] = value.astype(BF)
    wide, part = outer.shape
    own = pl.ds(pl.multiple_of((scalars[1] // 2) * part, part), part)
    outer[...] = sum(
        mine[pl.ds(c * wide, wide), own] + came[pl.ds(c * wide, wide), own].astype(F32)
        for c in range(copies)
    )


def halve_kernel(bit, scalars, mine, came, total, sent, whole):
    whole[...] = mine[...] + came[...].astype(F32)
    half = total.shape[1]
    side = (scalars[1] // bit) % 2
    total[...] = whole[:, pl.ds(pl.multiple_of(side * half, half), half)]
    sent[...] = whole[:, pl.ds(pl.multiple_of((1 - side) * half, half), half)].astype(BF)


def result_kernel(scale, outer, mine, came, result):
    result[...] = (scale * (outer[...] - (mine[...] + came[...].astype(F32)))).astype(BF)


def place_kernel(order, scalars, *refs):
    blocks, out = refs[:-1], refs[-1]
    me = scalars[0]
    wide = blocks[0].shape[0]
    flat = []
    for ref in blocks:
        flat += [ref[pl.ds(row, wide), :].astype(F32) for row in range(0, ref.shape[0], wide)]
    where = {r: flat[i] for i, r in enumerate(order)}
    for r in order:
        if r % 2:
            continue
        low, high = where[r], where[r ^ 1]
        odd = me % 2 == 1
        pair = jnp.concatenate([jnp.where(odd, high, low), jnp.where(odd, low, high)], 0)
        columns = pl.ds(pl.multiple_of(((me ^ r) // 2) * 128, 128), 128)
        out[:, columns] = pair.T


def run(kernel, scalars, arrays, outs, scratch=()):
    nbytes = sum(a.size * a.dtype.itemsize for a in arrays)
    nbytes += sum(s[0] * s[1] * jnp.dtype(t).itemsize for s, t in outs)
    smem = pl.BlockSpec(memory_space=pltpu.SMEM)
    vmem = pl.BlockSpec(memory_space=pltpu.VMEM)
    return pl.pallas_call(
        kernel,
        out_shape=[jax.ShapeDtypeStruct(s, t) for s, t in outs],
        in_specs=[smem] * len(scalars) + [vmem] * len(arrays),
        out_specs=[vmem] * len(outs),
        scratch_shapes=[pltpu.VMEM(s, t) for s, t in scratch],
        compiler_params=pltpu.CompilerParams(vmem_limit_bytes=nbytes + (8 << 20)),
    )(*scalars, *arrays)


def local(tokens, upstream, value_weight, forget_label, copy_index, adv_rate):
    dp, fsdp = lax.axis_size("dp"), lax.axis_size("fsdp")
    rows, features = tokens.shape
    outs = upstream.shape[1]
    wide = outs // dp
    part = features // fsdp
    pairs = fsdp // 2
    copies = adv_rate.shape[0]
    seq_length = rows * fsdp
    me = lax.axis_index("dp").astype(jnp.int32)
    quarter = lax.axis_index("fsdp").astype(jnp.int32)
    scalars = jnp.stack([me, quarter, forget_label[0], copy_index[0]])
    dp_bits = bits_of(dp)[::-1]
    far_bits = bits_of(fsdp)[1:]
    up_bits = dp_bits[::-1]
    up_bits = up_bits[1:2] + up_bits[:1] + up_bits[2:]
    strides = [2 ** sum(low < bit for low in up_bits[i:]) for i, bit in enumerate(up_bits)]

    def side_of(bit):
        return lambda me: (me // bit) % 2

    weight, up, labels, sent = run(
        functools.partial(prepare_kernel, wide, side_of(up_bits[0]), strides[0]),
        [scalars],
        [upstream, value_weight],
        [((wide, part), BF), ((outs, rows), BF), ((16, rows), BF), ((outs // 2 + 16, rows), BF)],
        [((128, part), F32)],
    )

    half_rows = rows // 2
    first = {0: tokens[:half_rows]}
    second = {0: tokens[half_rows:]}
    near = [swap(tokens, "dp", 1)]
    whole = {1: near[0]}

    def send(value, bit, *others):
        if bit == 1:
            others += (near[max(len(near) - 2, 0)],)
        if others:
            value = after(value, *others)
        came = swap(value, "dp", bit)
        if bit == 1:
            near.append(came)
        return came

    ties = ()
    top_bit = dp_bits[0]
    for step, up_bit in enumerate(up_bits, 1):
        if step == len(dp_bits) and step > 1:
            sent = after(sent, second[top_bit])
        came_up = swap(sent, "dp", up_bit)
        ready = [r for r in range(2, dp) if bin(r).count("1") == step]
        firsts, seconds = {}, {}
        for r in ready:
            bit = r & -r
            way = 2 * bit if r == dp - 1 and dp > 2 else bit
            firsts[r] = send(first[r ^ way], way, *(ties if way == 1 else ()))
        for r in ready:
            bit = r & -r
            others = (firsts[r],) if step == 1 else (came_up,) if step == 2 and bit == 1 else ()
            seconds[r] = send(second[r ^ bit], bit, *others)
        first.update(firsts)
        second.update(seconds)
        ties = (came_up,) if step == 1 else ()
        high, long = up.shape[0] // 2, 2 * up.shape[1]
        shapes = [((high, long), BF), ((16, long), BF)]
        if step < len(dp_bits):
            shapes.append(((high // 2 + 16, long), BF))
        following = (side_of(up_bits[step]), strides[step]) if step < len(dp_bits) else (None, None)
        joined = run(
            functools.partial(join_kernel, wide, side_of(up_bit), strides[step - 1], *following),
            [scalars],
            [up, labels, came_up],
            shapes,
        )
        up, labels = joined[:2]
        sent = joined[-1]
    order = [0]
    for bit in up_bits:
        order = order + [r ^ bit for r in order]
    late = [r for r in range(dp) if r & dp_bits[0] and r & 1]
    early = [r for r in range(dp) if r not in late]

    def pieces_of(blocks):
        return [x for r in blocks for x in ([whole[r]] if r in whole else [first[r], second[r]])]

    weight = after(weight, first[dp_bits[0]])
    for bit in bits_of(fsdp):
        weight = jnp.concatenate([weight, swap(weight, "fsdp", bit)])

    def total(send, keep, bits):
        shape = keep.shape
        came = swap(send, "fsdp", 1)
        for bit in bits:
            keep, sent = run(add_kernel, [], [keep, came], [(shape, F32), (shape, BF)])
            came = swap(sent, "fsdp", bit)
        return keep, came

    sizes = (part, pairs, copies, seq_length)
    stacked = (copies * wide, features // 2)

    def put_together(blocks, before):
        count = len(blocks) * rows
        shapes = [((count, features), BF), ((wide, count), BF), ((16, count), BF), ((wide, count), F32)]
        shapes += [(stacked, BF if before else F32), (stacked, F32)]
        places = [order.index(r) for r in blocks]
        return run(
            functools.partial(first_kernel, sizes, places, bool(before)),
            [scalars],
            pieces_of(blocks) + [up, labels, weight] + before,
            shapes,
        )

    *tokens_early, primal_early, sums, keep = put_together(early, [])
    *tokens_late, primal_late, send, keep = put_together(late, [sums, keep])
    (attacked,) = run(
        functools.partial(attack_kernel, copies),
        [scalars, adv_rate],
        [*total(send, keep, far_bits), weight],
        [(stacked, BF)],
    )
    send, keep = run(
        functools.partial(second_kernel, sizes),
        [scalars],
        [*tokens_early, *tokens_late, attacked, swap(attacked, "fsdp", 1)],
        [(stacked, BF), (stacked, F32)],
        [(stacked, F32)],
    )
    tangent, outer = run(
        functools.partial(tangent_kernel, copies),
        [scalars],
        [*total(send, keep, far_bits)],
        [(stacked, BF), ((wide, part), F32)],
    )
    send, keep = run(
        functools.partial(third_kernel, sizes),
        [scalars, adv_rate],
        [*tokens_early, primal_early, *tokens_late, primal_late, tangent, swap(tangent, "fsdp", 1)],
        [((wide, features // 2), BF), ((wide, features // 2), F32)],
        [((wide, features // 2), F32)],
    )

    came = swap(send, "fsdp", 1)
    for bit in far_bits[::-1]:
        shape = (wide, keep.shape[1] // 2)
        keep, sent = run(
            functools.partial(halve_kernel, bit),
            [scalars],
            [keep, came],
            [(shape, F32), (shape, BF)],
            [(keep.shape, F32)],
        )
        came = swap(sent, "fsdp", bit)
    scale = (float(seq_length) / float(dp)) ** 0.5
    (result,) = run(
        functools.partial(result_kernel, scale), [], [outer, keep, came], [((wide, part), BF)]
    )
    blocks = [result]
    came_order = [0]
    for r in range(dp - 1, 0, -1):
        came_order.append(r)
        blocks.append(swap(result, "dp", r))
    if 2 * wide == 128:
        (placed,) = run(
            functools.partial(place_kernel, came_order), [scalars], blocks, [((part, outs), F32)]
        )
        return placed
    result = jnp.concatenate(blocks).reshape(dp, wide, part)
    result = result[jnp.argsort(me ^ jnp.array(came_order))]
    return result.reshape(outs, part).T.astype(F32)


def solution(mesh):
    in_specs = (
        P(("dp", "fsdp"), None),
        P(("dp", "fsdp"), None),
        P("fsdp", None),
        P("dp"),
        P("dp"),
        P(),
    )
    out_specs = P("fsdp", None)
    return jax.shard_map(local, mesh=mesh, in_specs=in_specs, out_specs=out_specs, check_vma=False)
```

```python
import functools

import jax
import jax.numpy as jnp
from jax import lax
from jax.experimental import pallas as pl
from jax.experimental.pallas import tpu as pltpu
from jax.sharding import PartitionSpec as P

BF = jnp.bfloat16
F32 = jnp.float32


def first_slope(value):
    sig = jax.nn.sigmoid(value)
    return sig * (1.0 + value * (1.0 - sig))


def second_slope(value):
    sig = jax.nn.sigmoid(value)
    return sig * (1.0 - sig) * (2.0 + value * (1.0 - 2.0 * sig))


def swap(value, axis, bit):
    return lax.ppermute(value, axis, [(i, i ^ bit) for i in range(lax.axis_size(axis))])


def after(value, *others):
    return lax.optimization_barrier((value,) + others)[0]


def bits_of(size):
    found = []
    bit = 1
    while bit < size:
        found.append(bit)
        bit *= 2
    return found


def onehots(labels, copies):
    copy = labels[1:2, :].astype(F32)
    return [(copy == float(c)).astype(F32) for c in range(copies)]


def times_tokens(core, part, pairs, mine, other, held, rows):
    total = None
    for j in range(pairs):
        for value, side in ((mine, core), (other, 1 - core)):
            columns = pl.ds(pl.multiple_of((2 * j + side) * part, part), part)
            term = lax.dot_general(
                value[:, pl.ds(j * part, part)],
                held[rows, columns],
                (((1,), (1,)), ((), ())),
                preferred_element_type=F32,
            )
            total = term if total is None else total + term
    return total


def contract(core, part, pairs, delta, held, rows, send, keep, before):
    for j in range(pairs):
        place = pl.ds(j * part, part)
        for k, (out, side) in enumerate(((send, 1 - core), (keep, core))):
            columns = pl.ds(pl.multiple_of((2 * j + side) * part, part), part)
            term = jnp.dot(delta, held[rows, columns], preferred_element_type=F32)
            if before is not None:
                term = before[k][:, place] + term
            out[:, place] = term.astype(out.dtype)


def in_tiles(held, sums, keep, body):
    tile = min(held.shape[0], 1024)
    if held.shape[0] == tile:
        body(pl.ds(0, tile), None)
        return
    sums[...] = jnp.zeros_like(sums)
    keep[...] = jnp.zeros_like(keep)

    def step(i, none):
        body(pl.ds(pl.multiple_of(i * tile, tile), tile), (sums, keep))

    lax.fori_loop(0, held.shape[0] // tile, step, None)


def of_copy(value, hots):
    wide = value.shape[0] // len(hots)
    return sum(value[c * wide : (c + 1) * wide] * hot for c, hot in enumerate(hots))


def by_copy(delta, hots):
    delta = delta.astype(F32)
    return jnp.concatenate([delta * hot for hot in hots], 0).astype(BF)


def prepare_kernel(wide, side_of, stride, scalars, upstream, value_weight, weight, up, labels, sent, turned):
    me = scalars[0]
    group = 128 // wide
    columns = pl.ds(pl.multiple_of((me // group) * 128, 128), 128)
    turned[...] = value_weight[:, columns].astype(F32).T
    own = pl.ds(pl.multiple_of((me % group) * wide, wide), wide)
    weight[...] = turned[own, :].astype(BF)
    up[...] = upstream[...].astype(F32).T.astype(BF)
    row = lax.broadcasted_iota(jnp.int32, labels.shape, 0)
    both = jnp.where(row == 0, scalars[2], jnp.where(row == 1, scalars[3], 0))
    labels[...] = both.astype(F32).astype(BF)
    every_second(up, 1 - side_of(me), stride, wide, sent)
    sent[pl.ds(up.shape[0] // 2, 16), :] = labels[...]


def every_second(source, side, stride, wide, target, columns=slice(None)):
    for k in range(source.shape[0] // wide // 2):
        place = (2 * (k // stride) + side) * stride + k % stride
        block = pl.ds(pl.multiple_of(place * wide, wide), wide)
        target[pl.ds(k * wide, wide), columns] = source[block, :]


def join_kernel(wide, side_of, stride, next_side, next_stride, scalars, up, labels, came, new_up, new_labels, *sent):
    me = scalars[0]
    half, long = up.shape[0] // 2, up.shape[1]
    every_second(up, side_of(me), stride, wide, new_up, pl.ds(0, long))
    new_up[:, pl.ds(long, long)] = came[pl.ds(0, half), :]
    new_labels[:, pl.ds(0, long)] = labels[...]
    new_labels[:, pl.ds(long, long)] = came[pl.ds(half, 16), :]
    if sent:
        every_second(new_up, 1 - next_side(me), next_stride, wide, sent[0])
        sent[0][pl.ds(half // 2, 16), :] = new_labels[...]


def first_kernel(sizes, places, last, scalars, *refs):
    part, pairs, copies, length = sizes
    refs, outs = refs[:-6], refs[-6:]
    before, refs = (refs[-2:], refs[:-2]) if last else (None, refs)
    pieces, (all_up, all_labels, weight) = refs[:-3], refs[-3:]
    held, up, labels, primal_out, sums, keep = outs
    quarter = scalars[1]
    wide = up.shape[0]
    row = 0
    for piece in pieces:
        held[pl.ds(row, piece.shape[0]), :] = piece[...]
        row += piece.shape[0]
    rows = held.shape[0] // len(places)
    for i, place in enumerate(places):
        up[:, pl.ds(i * rows, rows)] = all_up[:, pl.ds(place * rows, rows)]
        labels[:, pl.ds(i * rows, rows)] = all_labels[:, pl.ds(place * rows, rows)]

    def body(rows, prior):
        primal = None
        for i in range(2 * pairs):
            columns = pl.ds(pl.multiple_of((quarter ^ i) * part, part), part)
            term = lax.dot_general(
                weight[pl.ds(i * wide, wide), :],
                held[rows, columns],
                (((1,), (1,)), ((), ())),
                preferred_element_type=F32,
            )
            primal = term if primal is None else primal + term
        primal_out[:, rows] = primal
        hots = onehots(labels[:, rows], copies)
        forget = labels[0:1, rows].astype(F32)
        delta = (forget * up[:, rows].astype(F32) * first_slope(primal) / length).astype(BF)
        contract(quarter % 2, part, pairs, by_copy(delta, hots), held, rows, sums, keep, prior)

    if last:
        body(pl.ds(0, held.shape[0]), before)
    else:
        in_tiles(held, sums, keep, body)


def sort_kernel(sizes, rows, scalars, rate, *refs):
    part, pairs, copies, length = sizes
    early, late, (own, own_side, sent, sent_side) = refs[:4], refs[4:8], refs[8:]
    core = scalars[1] % 2
    wide = late[1].shape[0]
    counts = [jnp.int32(0), jnp.int32(0)]
    for held, up, labels, primal in (early, late):
        for i in range(held.shape[0] // rows):
            place = pl.ds(i * rows, rows)
            label = labels[:, place].astype(F32)
            forget, copy = label[0:1, :], label[1:2, :]
            upward = up[:, place].astype(F32)
            own_rate = sum((copy == float(c)).astype(F32) * rate[c] for c in range(copies))
            factor = own_rate * (forget * upward * second_slope(primal[:, place]) / length)
            signed = (1.0 - 2.0 * forget) * upward
            mine = (jnp.max(copy).astype(jnp.int32) == core).astype(jnp.int32)
            for k, (tokens, side) in enumerate(((own, own_side), (sent, sent_side))):
                at = pl.ds(pl.multiple_of(counts[k] * rows, rows), rows)
                here = mine if k == 0 else 1 - mine

                @pl.when(here == 1)
                def _(tokens=tokens, side=side, at=at):
                    tokens[at, :] = held[place, :]
                    side[pl.ds(0, wide), at] = signed.astype(BF)
                    side[pl.ds(wide, wide), at] = factor.astype(BF)

                counts[k] = counts[k] + here


def in_tiles_of(parts, out, body):
    tile = min(parts[0][0].shape[0], 1024)
    if parts[0][0].shape[0] == tile:
        for i, tokens in enumerate(parts):
            body(tokens, pl.ds(0, tile), out, i > 0)
        return
    out[...] = jnp.zeros_like(out)
    for tokens in parts:

        def step(i, none):
            body(tokens, pl.ds(pl.multiple_of(i * tile, tile), tile), out, True)

        lax.fori_loop(0, tokens[0].shape[0] // tile, step, None)


def add_terms(delta, held, rows, out, more):
    term = jnp.dot(delta, held[rows, :], preferred_element_type=F32)
    out[...] = out[...] + term if more else term


def second_kernel(sizes, scalars, *refs):
    part, pairs, copies, length = sizes
    early, late, (mine, other, send, keep) = refs[:2], refs[2:4], refs[4:]
    core = scalars[1] % 2

    def body(tokens, rows, keep, more):
        held, side = tokens
        altered = times_tokens(core, part, pairs, mine, other, held, rows)
        upward = side[pl.ds(0, altered.shape[0]), rows].astype(F32)
        delta = (upward * first_slope(altered) / length).astype(BF)
        add_terms(delta, held, rows, keep, more)

    in_tiles_of((early, late), keep, body)
    send[...] = keep[...].astype(BF)


def third_kernel(sizes, scalars, *refs):
    part, pairs, copies, length = sizes
    early, late, (local, summed, came, send, keep, tangent, curv) = refs[:2], refs[2:4], refs[4:]
    core = scalars[1] % 2
    tangent[...] = (summed[...] + came[...].astype(F32)).astype(BF)

    def body(tokens, rows, curv, more):
        held, side = tokens
        forward = lax.dot_general(
            tangent[...], held[rows, :], (((1,), (1,)), ((), ())), preferred_element_type=F32
        )
        wide = forward.shape[0]
        delta = (side[pl.ds(wide, wide), rows].astype(F32) * forward).astype(BF)
        add_terms(delta, held, rows, curv, more)

    in_tiles_of((early, late), curv, body)
    for j in range(pairs):
        for out, side in ((send, 1 - core), (keep, core)):
            columns = pl.ds(pl.multiple_of((2 * j + side) * part, part), part)
            value = local[:, columns] - curv[:, columns]
            out[:, pl.ds(j * part, part)] = value.astype(out.dtype)


def add_kernel(mine, came, total, sent):
    value = mine[...] + came[...].astype(F32)
    total[...] = value
    sent[...] = value.astype(BF)


def attack_kernel(scalars, rate, mine, came, weight, own, sent):
    quarter = scalars[1]
    part = weight.shape[1]
    wide = own.shape[0]
    for j in range(mine.shape[1] // part):
        place = quarter ^ (2 * j + quarter % 2)
        start = weight[pl.ds(pl.multiple_of(place * wide, wide), wide), :].astype(F32)
        columns = pl.ds(j * part, part)
        for out, c in ((own, quarter % 2), (sent, 1 - quarter % 2)):
            rows = pl.ds(pl.multiple_of(c * wide, wide), wide)
            grad = mine[rows, columns] + came[rows, columns].astype(F32)
            out[:, columns] = (start - rate[c] * grad).astype(BF)


def halve_kernel(bit, scalars, mine, came, total, sent, whole):
    whole[...] = mine[...] + came[...].astype(F32)
    half = total.shape[1]
    side = (scalars[1] // bit) % 2
    total[...] = whole[:, pl.ds(pl.multiple_of(side * half, half), half)]
    sent[...] = whole[:, pl.ds(pl.multiple_of((1 - side) * half, half), half)].astype(BF)


def result_kernel(scale, mine, came, result):
    result[...] = (scale * (mine[...] + came[...].astype(F32))).astype(BF)


def place_kernel(order, scalars, *refs):
    blocks, out = refs[:-1], refs[-1]
    me = scalars[0]
    wide = blocks[0].shape[0]
    flat = []
    for ref in blocks:
        flat += [ref[pl.ds(row, wide), :].astype(F32) for row in range(0, ref.shape[0], wide)]
    where = {r: flat[i] for i, r in enumerate(order)}
    for r in order:
        if r % 2:
            continue
        low, high = where[r], where[r ^ 1]
        odd = me % 2 == 1
        pair = jnp.concatenate([jnp.where(odd, high, low), jnp.where(odd, low, high)], 0)
        columns = pl.ds(pl.multiple_of(((me ^ r) // 2) * 128, 128), 128)
        out[:, columns] = pair.T


def run(kernel, scalars, arrays, outs, scratch=()):
    nbytes = sum(a.size * a.dtype.itemsize for a in arrays)
    nbytes += sum(s[0] * s[1] * jnp.dtype(t).itemsize for s, t in outs)
    smem = pl.BlockSpec(memory_space=pltpu.SMEM)
    vmem = pl.BlockSpec(memory_space=pltpu.VMEM)
    return pl.pallas_call(
        kernel,
        out_shape=[jax.ShapeDtypeStruct(s, t) for s, t in outs],
        in_specs=[smem] * len(scalars) + [vmem] * len(arrays),
        out_specs=[vmem] * len(outs),
        scratch_shapes=[pltpu.VMEM(s, t) for s, t in scratch],
        compiler_params=pltpu.CompilerParams(vmem_limit_bytes=nbytes + (8 << 20)),
    )(*scalars, *arrays)


def local(tokens, upstream, value_weight, forget_label, copy_index, adv_rate):
    dp, fsdp = lax.axis_size("dp"), lax.axis_size("fsdp")
    rows, features = tokens.shape
    outs = upstream.shape[1]
    wide = outs // dp
    part = features // fsdp
    pairs = fsdp // 2
    copies = adv_rate.shape[0]
    seq_length = rows * fsdp
    me = lax.axis_index("dp").astype(jnp.int32)
    quarter = lax.axis_index("fsdp").astype(jnp.int32)
    scalars = jnp.stack([me, quarter, forget_label[0], copy_index[0]])
    dp_bits = bits_of(dp)[::-1]
    far_bits = bits_of(fsdp)[1:]
    up_bits = dp_bits[::-1]
    up_bits = up_bits[1:2] + up_bits[:1] + up_bits[2:]
    strides = [2 ** sum(low < bit for low in up_bits[i:]) for i, bit in enumerate(up_bits)]

    def side_of(bit):
        return lambda me: (me // bit) % 2

    weight, up, labels, sent = run(
        functools.partial(prepare_kernel, wide, side_of(up_bits[0]), strides[0]),
        [scalars],
        [upstream, value_weight],
        [((wide, part), BF), ((outs, rows), BF), ((16, rows), BF), ((outs // 2 + 16, rows), BF)],
        [((128, part), F32)],
    )

    half_rows = rows // 2
    first = {0: tokens[:half_rows]}
    second = {0: tokens[half_rows:]}
    near = [swap(tokens, "dp", 1)]
    whole = {1: near[0]}

    def send(value, bit, *others):
        if bit == 1:
            others += (near[max(len(near) - 2, 0)],)
        if others:
            value = after(value, *others)
        came = swap(value, "dp", bit)
        if bit == 1:
            near.append(came)
        return came

    ties = ()
    top_bit = dp_bits[0]
    for step, up_bit in enumerate(up_bits, 1):
        if step == len(dp_bits) and step > 1:
            sent = after(sent, second[top_bit])
        came_up = swap(sent, "dp", up_bit)
        ready = [r for r in range(2, dp) if bin(r).count("1") == step]
        firsts, seconds = {}, {}
        for r in ready:
            bit = r & -r
            way = 2 * bit if r == dp - 1 and dp > 2 else bit
            firsts[r] = send(first[r ^ way], way, *(ties if way == 1 else ()))
        for r in ready:
            bit = r & -r
            others = (firsts[r],) if step == 1 else (came_up,) if step == 2 and bit == 1 else ()
            seconds[r] = send(second[r ^ bit], bit, *others)
        first.update(firsts)
        second.update(seconds)
        ties = (came_up,) if step == 1 else ()
        high, long = up.shape[0] // 2, 2 * up.shape[1]
        shapes = [((high, long), BF), ((16, long), BF)]
        if step < len(dp_bits):
            shapes.append(((high // 2 + 16, long), BF))
        following = (side_of(up_bits[step]), strides[step]) if step < len(dp_bits) else (None, None)
        joined = run(
            functools.partial(join_kernel, wide, side_of(up_bit), strides[step - 1], *following),
            [scalars],
            [up, labels, came_up],
            shapes,
        )
        up, labels = joined[:2]
        sent = joined[-1]
    order = [0]
    for bit in up_bits:
        order = order + [r ^ bit for r in order]
    late = [r for r in range(dp) if r & dp_bits[0] and r & 1]
    early = [r for r in range(dp) if r not in late]

    def pieces_of(blocks):
        return [x for r in blocks for x in ([whole[r]] if r in whole else [first[r], second[r]])]

    weight = after(weight, first[dp_bits[0]])
    for bit in bits_of(fsdp):
        weight = jnp.concatenate([weight, swap(weight, "fsdp", bit)])

    def total(keep, came, bits):
        for bit in bits:
            keep, sent = run(add_kernel, [], [keep, came], [(keep.shape, F32), (keep.shape, BF)])
            came = swap(sent, "fsdp", bit)
        return keep, came

    sizes = (part, pairs, copies, seq_length)
    stacked = (copies * wide, features // 2)

    def put_together(blocks, before):
        count = len(blocks) * rows
        shapes = [((count, features), BF), ((wide, count), BF), ((16, count), BF), ((wide, count), F32)]
        shapes += [(stacked, BF if before else F32), (stacked, F32)]
        places = [order.index(r) for r in blocks]
        return run(
            functools.partial(first_kernel, sizes, places, bool(before)),
            [scalars],
            pieces_of(blocks) + [up, labels, weight] + before,
            shapes,
        )

    *tokens_early, primal_early, sums, keep = put_together(early, [])
    *tokens_late, primal_late, send, keep = put_together(late, [sums, keep])
    summed, came = total(keep, swap(send, "fsdp", 1), far_bits)
    tokens_early[2] = after(tokens_early[2], summed)
    taken = ((dp // 2 * rows, features), BF)
    beside = ((2 * wide, dp // 2 * rows), BF)
    own, own_side, sent, sent_side = run(
        functools.partial(sort_kernel, sizes, rows),
        [scalars, adv_rate],
        [*tokens_early, primal_early, *tokens_late, primal_late],
        [taken, beside, taken, beside],
    )
    mine = [own, own_side, swap(sent, "fsdp", 1), swap(sent_side, "fsdp", 1)]
    half, full = (wide, features // 2), (wide, features)
    attacked, sent = run(
        attack_kernel, [scalars, adv_rate], [summed, came, weight], [(half, BF), (half, BF)]
    )
    send, keep = run(
        functools.partial(second_kernel, sizes),
        [scalars],
        [*mine, attacked, swap(sent, "fsdp", 1)],
        [(full, BF), (full, F32)],
    )
    send, keep = run(
        functools.partial(third_kernel, sizes),
        [scalars],
        [*mine, keep, *total(keep, swap(send, "fsdp", far_bits[0]), far_bits[1:])],
        [(half, BF), (half, F32)],
        [(full, BF), (full, F32)],
    )

    came = swap(send, "fsdp", 1)
    for bit in far_bits[::-1]:
        shape = (wide, keep.shape[1] // 2)
        keep, sent = run(
            functools.partial(halve_kernel, bit),
            [scalars],
            [keep, came],
            [(shape, F32), (shape, BF)],
            [(keep.shape, F32)],
        )
        came = swap(sent, "fsdp", bit)
    scale = (float(seq_length) / float(dp)) ** 0.5
    (result,) = run(
        functools.partial(result_kernel, scale), [], [keep, came], [((wide, part), BF)]
    )
    blocks = [result]
    came_order = [0]
    for r in range(dp - 1, 0, -1):
        came_order.append(r)
        blocks.append(swap(result, "dp", r))
    if 2 * wide == 128:
        (placed,) = run(
            functools.partial(place_kernel, came_order), [scalars], blocks, [((part, outs), F32)]
        )
        return placed
    result = jnp.concatenate(blocks).reshape(dp, wide, part)
    result = result[jnp.argsort(me ^ jnp.array(came_order))]
    return result.reshape(outs, part).T.astype(F32)


def solution(mesh):
    in_specs = (
        P(("dp", "fsdp"), None),
        P(("dp", "fsdp"), None),
        P("fsdp", None),
        P("dp"),
        P("dp"),
        P(),
    )
    out_specs = P("fsdp", None)
    return jax.shard_map(local, mesh=mesh, in_specs=in_specs, out_specs=out_specs, check_vma=False)
```

```python
import functools

import jax
import jax.numpy as jnp
from jax import lax
from jax.experimental import pallas as pl
from jax.experimental.pallas import tpu as pltpu
from jax.sharding import PartitionSpec as P

BF = jnp.bfloat16
F32 = jnp.float32


def first_slope(value):
    sig = jax.nn.sigmoid(value)
    return sig * (1.0 + value * (1.0 - sig))


def second_slope(value):
    sig = jax.nn.sigmoid(value)
    return sig * (1.0 - sig) * (2.0 + value * (1.0 - 2.0 * sig))


def swap(value, axis, bit):
    return lax.ppermute(value, axis, [(i, i ^ bit) for i in range(lax.axis_size(axis))])


def after(value, *others):
    return lax.optimization_barrier((value,) + others)[0]


def bits_of(size):
    found = []
    bit = 1
    while bit < size:
        found.append(bit)
        bit *= 2
    return found


def onehots(labels, copies):
    copy = labels[1:2, :].astype(F32)
    return [(copy == float(c)).astype(F32) for c in range(copies)]


def times_tokens(core, part, pairs, mine, other, held, rows):
    total = None
    for j in range(pairs):
        for value, side in ((mine, core), (other, 1 - core)):
            columns = pl.ds(pl.multiple_of((2 * j + side) * part, part), part)
            term = lax.dot_general(
                value[:, pl.ds(j * part, part)],
                held[rows, columns],
                (((1,), (1,)), ((), ())),
                preferred_element_type=F32,
            )
            total = term if total is None else total + term
    return total


def contract(core, part, pairs, delta, held, rows, send, keep, before):
    for j in range(pairs):
        place = pl.ds(j * part, part)
        for k, (out, side) in enumerate(((send, 1 - core), (keep, core))):
            columns = pl.ds(pl.multiple_of((2 * j + side) * part, part), part)
            term = jnp.dot(delta, held[rows, columns], preferred_element_type=F32)
            if before is not None:
                term = before[k][:, place] + term
            out[:, place] = term.astype(out.dtype)


def by_copy(delta, hots):
    delta = delta.astype(F32)
    return jnp.concatenate([delta * hot for hot in hots], 0).astype(BF)


def prepare_kernel(wide, side_of, stride, scalars, upstream, value_weight, weight, up, labels, sent, turned):
    me = scalars[0]
    group = 128 // wide
    columns = pl.ds(pl.multiple_of((me // group) * 128, 128), 128)
    turned[...] = value_weight[:, columns].astype(F32).T
    own = pl.ds(pl.multiple_of((me % group) * wide, wide), wide)
    weight[...] = turned[own, :].astype(BF)
    up[...] = upstream[...].astype(F32).T.astype(BF)
    row = lax.broadcasted_iota(jnp.int32, labels.shape, 0)
    both = jnp.where(row == 0, scalars[2], jnp.where(row == 1, scalars[3], 0))
    labels[...] = both.astype(F32).astype(BF)
    every_second(up, 1 - side_of(me), stride, wide, sent)
    sent[pl.ds(up.shape[0] // 2, 16), :] = labels[...]


def every_second(source, side, stride, wide, target, columns=slice(None)):
    for k in range(source.shape[0] // wide // 2):
        place = (2 * (k // stride) + side) * stride + k % stride
        block = pl.ds(pl.multiple_of(place * wide, wide), wide)
        target[pl.ds(k * wide, wide), columns] = source[block, :]


def join_kernel(wide, side_of, stride, next_side, next_stride, scalars, up, labels, came, new_up, new_labels, *sent):
    me = scalars[0]
    half, long = up.shape[0] // 2, up.shape[1]
    every_second(up, side_of(me), stride, wide, new_up, pl.ds(0, long))
    new_up[:, pl.ds(long, long)] = came[pl.ds(0, half), :]
    new_labels[:, pl.ds(0, long)] = labels[...]
    new_labels[:, pl.ds(long, long)] = came[pl.ds(half, 16), :]
    if sent:
        every_second(new_up, 1 - next_side(me), next_stride, wide, sent[0])
        sent[0][pl.ds(half // 2, 16), :] = new_labels[...]


def put_together(pieces, held):
    row = 0
    for piece in pieces:
        held[pl.ds(row, piece.shape[0]), :] = piece[...]
        row += piece.shape[0]


def times_weight(quarter, part, weight, held, rows):
    wide = weight.shape[0] * part // held.shape[1]
    total = None
    for i in range(weight.shape[0] // wide):
        columns = pl.ds(pl.multiple_of((quarter ^ i) * part, part), part)
        term = lax.dot_general(
            weight[pl.ds(i * wide, wide), :],
            held[rows, columns],
            (((1,), (1,)), ((), ())),
            preferred_element_type=F32,
        )
        total = term if total is None else total + term
    return total


def tiles_of(held, body):
    tile = min(held.shape[0], 1024)
    if held.shape[0] == tile:
        body(pl.ds(0, tile), False)
        return

    def step(i, none):
        body(pl.ds(pl.multiple_of(i * tile, tile), tile), True)

    lax.fori_loop(0, held.shape[0] // tile, step, None)


def primal_kernel(part, scalars, *refs):
    pieces, (weight, held, primal) = refs[:-3], refs[-3:]
    put_together(pieces, held)

    def body(rows, _):
        primal[:, rows] = times_weight(scalars[1], part, weight, held, rows)

    tiles_of(held, body)


def first_kernel(sizes, places, scalars, *refs):
    part, pairs, copies, length = sizes
    pieces, refs = refs[:-12], refs[-12:]
    all_up, all_labels, weight, held_early, primal_early, *refs = refs
    held_late, primal_late, up, labels, send, keep, sums = refs
    quarter = scalars[1]
    put_together(pieces, held_late)
    primal_late[...] = times_weight(quarter, part, weight, held_late, pl.ds(0, held_late.shape[0]))
    rows = up.shape[1] // len(places)
    for i, place in enumerate(places):
        up[:, pl.ds(i * rows, rows)] = all_up[:, pl.ds(place * rows, rows)]
        labels[:, pl.ds(i * rows, rows)] = all_labels[:, pl.ds(place * rows, rows)]

    def terms(held, primal, rows, start, send, before):
        lanes = pl.ds(start + rows.start, rows.size)
        hots = onehots(labels[:, lanes], copies)
        forget = labels[0:1, lanes].astype(F32)
        slope = first_slope(primal[:, rows])
        delta = (forget * up[:, lanes].astype(F32) * slope / length).astype(BF)
        contract(quarter % 2, part, pairs, by_copy(delta, hots), held, rows, send, keep, before)

    if held_early.shape[0] > 1024:
        sums[...] = jnp.zeros_like(sums)
        keep[...] = jnp.zeros_like(keep)

    def body(rows, more):
        terms(held_early, primal_early, rows, 0, sums, (sums, keep) if more else None)

    tiles_of(held_early, body)
    every = pl.ds(0, held_late.shape[0])
    terms(held_late, primal_late, every, held_early.shape[0], send, (sums, keep))


def sort_kernel(sizes, rows, scalars, rate, *refs):
    part, pairs, copies, length = sizes
    early, late, (up, labels, own, own_side, sent_side, *refs) = refs[:2], refs[2:4], refs[4:]
    pieces, sent = refs[:-1], refs[-1]
    core = scalars[1] % 2
    wide = up.shape[0]
    counts = [jnp.int32(0), jnp.int32(0)]
    start = 0
    for held, primal in (early, late):
        for i in range(held.shape[0] // rows):
            place = pl.ds(i * rows, rows)
            label = labels[:, pl.ds(start, rows)].astype(F32)
            forget, copy = label[0:1, :], label[1:2, :]
            upward = up[:, pl.ds(start, rows)].astype(F32)
            start += rows
            own_rate = sum((copy == float(c)).astype(F32) * rate[c] for c in range(copies))
            factor = own_rate * (forget * upward * second_slope(primal[:, place]) / length)
            signed = (1.0 - 2.0 * forget) * upward
            mine = (jnp.max(copy).astype(jnp.int32) == core).astype(jnp.int32)
            for k, (tokens, side) in enumerate(((own, own_side), (sent, sent_side))):
                at = pl.ds(pl.multiple_of(counts[k] * rows, rows), rows)
                here = mine if k == 0 else 1 - mine

                @pl.when(here == 1)
                def _(tokens=tokens, side=side, at=at):
                    tokens[at, :] = held[place, :]
                    side[pl.ds(0, wide), at] = signed.astype(BF)
                    side[pl.ds(wide, wide), at] = factor.astype(BF)

                counts[k] = counts[k] + here
    for i, piece in enumerate(pieces):
        piece[...] = sent[pl.ds(i * piece.shape[0], piece.shape[0]), :]


def in_tiles_of(parts, out, body):
    tile = min(parts[0][0].shape[0], 1024)
    if parts[0][0].shape[0] == tile:
        for i, tokens in enumerate(parts):
            body(tokens, pl.ds(0, tile), out, i > 0)
        return
    out[...] = jnp.zeros_like(out)
    for tokens in parts:

        def step(i, none):
            body(tokens, pl.ds(pl.multiple_of(i * tile, tile), tile), out, True)

        lax.fori_loop(0, tokens[0].shape[0] // tile, step, None)


def add_terms(delta, held, rows, out, more):
    term = jnp.dot(delta, held[rows, :], preferred_element_type=F32)
    out[...] = out[...] + term if more else term


def second_kernel(sizes, scalars, *refs):
    part, pairs, copies, length = sizes
    early, pieces, (side, mine, other, held, send, keep) = refs[:2], refs[2:-6], refs[-6:]
    late = (held, side)
    core = scalars[1] % 2
    put_together(pieces, held)

    def body(tokens, rows, keep, more):
        held, side = tokens
        altered = times_tokens(core, part, pairs, mine, other, held, rows)
        upward = side[pl.ds(0, altered.shape[0]), rows].astype(F32)
        delta = (upward * first_slope(altered) / length).astype(BF)
        add_terms(delta, held, rows, keep, more)

    in_tiles_of((early, late), keep, body)
    send[...] = keep[...].astype(BF)


def third_kernel(sizes, scalars, *refs):
    part, pairs, copies, length = sizes
    early, late, (local, summed, came, send, keep, tangent, curv) = refs[:2], refs[2:4], refs[4:]
    core = scalars[1] % 2
    tangent[...] = (summed[...] + came[...].astype(F32)).astype(BF)

    def body(tokens, rows, curv, more):
        held, side = tokens
        forward = lax.dot_general(
            tangent[...], held[rows, :], (((1,), (1,)), ((), ())), preferred_element_type=F32
        )
        wide = forward.shape[0]
        delta = (side[pl.ds(wide, wide), rows].astype(F32) * forward).astype(BF)
        add_terms(delta, held, rows, curv, more)

    in_tiles_of((early, late), curv, body)
    for j in range(pairs):
        for out, side in ((send, 1 - core), (keep, core)):
            columns = pl.ds(pl.multiple_of((2 * j + side) * part, part), part)
            value = local[:, columns] - curv[:, columns]
            out[:, pl.ds(j * part, part)] = value.astype(out.dtype)


def add_kernel(mine, came, total, sent):
    value = mine[...] + came[...].astype(F32)
    total[...] = value
    sent[...] = value.astype(BF)


def attack_kernel(scalars, rate, mine, came, weight, own, sent):
    quarter = scalars[1]
    part = weight.shape[1]
    wide = own.shape[0]
    for j in range(mine.shape[1] // part):
        place = quarter ^ (2 * j + quarter % 2)
        start = weight[pl.ds(pl.multiple_of(place * wide, wide), wide), :].astype(F32)
        columns = pl.ds(j * part, part)
        for out, c in ((own, quarter % 2), (sent, 1 - quarter % 2)):
            rows = pl.ds(pl.multiple_of(c * wide, wide), wide)
            grad = mine[rows, columns] + came[rows, columns].astype(F32)
            out[:, columns] = (start - rate[c] * grad).astype(BF)


def halve_kernel(bit, scalars, mine, came, total, sent, whole):
    whole[...] = mine[...] + came[...].astype(F32)
    half = total.shape[1]
    side = (scalars[1] // bit) % 2
    total[...] = whole[:, pl.ds(pl.multiple_of(side * half, half), half)]
    sent[...] = whole[:, pl.ds(pl.multiple_of((1 - side) * half, half), half)].astype(BF)


def result_kernel(scale, mine, came, result):
    result[...] = (scale * (mine[...] + came[...].astype(F32))).astype(BF)


def place_kernel(order, scalars, *refs):
    blocks, (out, joined) = refs[:-2], refs[-2:]
    me = scalars[0]
    wide = blocks[0].shape[0]
    for r, block in zip(order, blocks):
        joined[pl.ds(pl.multiple_of((me ^ r) * wide, wide), wide), :] = block[...]
    out[...] = joined[...].T.astype(F32)


def run(kernel, scalars, arrays, outs, scratch=()):
    nbytes = sum(a.size * a.dtype.itemsize for a in arrays)
    nbytes += sum(s[0] * s[1] * jnp.dtype(t).itemsize for s, t in outs)
    smem = pl.BlockSpec(memory_space=pltpu.SMEM)
    vmem = pl.BlockSpec(memory_space=pltpu.VMEM)
    return pl.pallas_call(
        kernel,
        out_shape=[jax.ShapeDtypeStruct(s, t) for s, t in outs],
        in_specs=[smem] * len(scalars) + [vmem] * len(arrays),
        out_specs=[vmem] * len(outs),
        scratch_shapes=[pltpu.VMEM(s, t) for s, t in scratch],
        compiler_params=pltpu.CompilerParams(vmem_limit_bytes=nbytes + (8 << 20)),
    )(*scalars, *arrays)


def local(tokens, upstream, value_weight, forget_label, copy_index, adv_rate):
    dp, fsdp = lax.axis_size("dp"), lax.axis_size("fsdp")
    rows, features = tokens.shape
    outs = upstream.shape[1]
    wide = outs // dp
    part = features // fsdp
    pairs = fsdp // 2
    copies = adv_rate.shape[0]
    seq_length = rows * fsdp
    me = lax.axis_index("dp").astype(jnp.int32)
    quarter = lax.axis_index("fsdp").astype(jnp.int32)
    scalars = jnp.stack([me, quarter, forget_label[0], copy_index[0]])
    dp_bits = bits_of(dp)[::-1]
    far_bits = bits_of(fsdp)[1:]
    up_bits = dp_bits[::-1]
    up_bits = up_bits[1:2] + up_bits[:1] + up_bits[2:]
    strides = [2 ** sum(low < bit for low in up_bits[i:]) for i, bit in enumerate(up_bits)]

    def side_of(bit):
        return lambda me: (me // bit) % 2

    weight, up, labels, sent = run(
        functools.partial(prepare_kernel, wide, side_of(up_bits[0]), strides[0]),
        [scalars],
        [upstream, value_weight],
        [((wide, part), BF), ((outs, rows), BF), ((16, rows), BF), ((outs // 2 + 16, rows), BF)],
        [((128, part), F32)],
    )

    half_rows = rows // 2
    first = {0: tokens[:half_rows]}
    second = {0: tokens[half_rows:]}
    near = [swap(tokens, "dp", 1)]
    whole = {1: near[0]}

    def send(value, bit, *others):
        if bit == 1:
            others += (near[max(len(near) - 2, 0)],)
        if others:
            value = after(value, *others)
        came = swap(value, "dp", bit)
        if bit == 1:
            near.append(came)
        return came

    ties = ()
    top_bit = dp_bits[0]
    for step, up_bit in enumerate(up_bits, 1):
        if step == len(dp_bits) and step > 1:
            sent = after(sent, second[top_bit])
        came_up = swap(sent, "dp", up_bit)
        ready = [r for r in range(2, dp) if bin(r).count("1") == step]
        firsts, seconds = {}, {}
        for r in ready:
            bit = r & -r
            way = 2 * bit if r == dp - 1 and dp > 2 else bit
            firsts[r] = send(first[r ^ way], way, *(ties if way == 1 else ()))
        for r in ready:
            bit = r & -r
            others = (firsts[r],) if step == 1 else (came_up,) if step == 2 and bit == 1 else ()
            seconds[r] = send(second[r ^ bit], bit, *others)
        first.update(firsts)
        second.update(seconds)
        ties = (came_up,) if step == 1 else ()
        high, long = up.shape[0] // 2, 2 * up.shape[1]
        shapes = [((high, long), BF), ((16, long), BF)]
        if step < len(dp_bits):
            shapes.append(((high // 2 + 16, long), BF))
        following = (side_of(up_bits[step]), strides[step]) if step < len(dp_bits) else (None, None)
        joined = run(
            functools.partial(join_kernel, wide, side_of(up_bit), strides[step - 1], *following),
            [scalars],
            [up, labels, came_up],
            shapes,
        )
        up, labels = joined[:2]
        sent = joined[-1]
    order = [0]
    for bit in up_bits:
        order = order + [r ^ bit for r in order]
    late = [r for r in range(dp) if r & dp_bits[0] and r & 1]
    early = [r for r in range(dp) if r not in late]

    def pieces_of(blocks):
        return [x for r in blocks for x in ([whole[r]] if r in whole else [first[r], second[r]])]

    weight = after(weight, first[dp_bits[0]])
    for bit in bits_of(fsdp):
        weight = jnp.concatenate([weight, swap(weight, "fsdp", bit)])

    def total(keep, came, bits):
        for bit in bits:
            keep, sent = run(add_kernel, [], [keep, came], [(keep.shape, F32), (keep.shape, BF)])
            came = swap(sent, "fsdp", bit)
        return keep, came

    sizes = (part, pairs, copies, seq_length)
    stacked = (copies * wide, features // 2)
    count = rows * len(early)
    held_early, primal_early = run(
        functools.partial(primal_kernel, part),
        [scalars],
        pieces_of(early) + [weight],
        [((count, features), BF), ((wide, count), F32)],
    )
    count = rows * len(late)
    held_late, primal_late, up, labels, send, keep = run(
        functools.partial(first_kernel, sizes, [order.index(r) for r in early + late]),
        [scalars],
        pieces_of(late) + [up, labels, weight, held_early, primal_early],
        [
            ((count, features), BF),
            ((wide, count), F32),
            ((wide, dp * rows), BF),
            ((16, dp * rows), BF),
            (stacked, BF),
            (stacked, F32),
        ],
        [(stacked, F32)],
    )
    summed, came = total(keep, swap(send, "fsdp", 1), far_bits)
    labels = after(labels, summed)
    taken = ((dp // 2 * rows, features), BF)
    beside = ((2 * wide, dp // 2 * rows), BF)
    cut = ((half_rows, features), BF)
    own, own_side, sent_side, *sent = run(
        functools.partial(sort_kernel, sizes, rows),
        [scalars, adv_rate],
        [held_early, primal_early, held_late, primal_late, up, labels],
        [taken, beside, beside] + [cut] * dp,
        [taken],
    )
    came_side = swap(sent_side, "fsdp", 1)
    came_pieces = [swap(piece, "fsdp", 1) for piece in sent]
    half, full = (wide, features // 2), (wide, features)
    attacked, sent = run(
        attack_kernel, [scalars, adv_rate], [summed, came, weight], [(half, BF), (half, BF)]
    )
    held, send, keep = run(
        functools.partial(second_kernel, sizes),
        [scalars],
        [own, own_side, *came_pieces, came_side, attacked, swap(sent, "fsdp", 1)],
        [taken, (full, BF), (full, F32)],
    )
    mine = [own, own_side, held, came_side]
    send, keep = run(
        functools.partial(third_kernel, sizes),
        [scalars],
        [*mine, keep, *total(keep, swap(send, "fsdp", far_bits[0]), far_bits[1:])],
        [(half, BF), (half, F32)],
        [(full, BF), (full, F32)],
    )

    came = swap(send, "fsdp", 1)
    for bit in far_bits[::-1]:
        shape = (wide, keep.shape[1] // 2)
        keep, sent = run(
            functools.partial(halve_kernel, bit),
            [scalars],
            [keep, came],
            [(shape, F32), (shape, BF)],
            [(keep.shape, F32)],
        )
        came = swap(sent, "fsdp", bit)
    scale = (float(seq_length) / float(dp)) ** 0.5
    (result,) = run(
        functools.partial(result_kernel, scale), [], [keep, came], [((wide, part), BF)]
    )
    came_order = sorted(range(dp), key=lambda r: format(r, f"0{len(dp_bits)}b")[::-1])
    blocks = [swap(result, "dp", r) if r else result for r in came_order]
    (placed,) = run(
        functools.partial(place_kernel, came_order),
        [scalars],
        blocks,
        [((part, outs), F32)],
        [((outs, part), BF)],
    )
    return placed


def solution(mesh):
    in_specs = (
        P(("dp", "fsdp"), None),
        P(("dp", "fsdp"), None),
        P("fsdp", None),
        P("dp"),
        P("dp"),
        P(),
    )
    out_specs = P("fsdp", None)
    return jax.shard_map(local, mesh=mesh, in_specs=in_specs, out_specs=out_specs, check_vma=False)
```

```python
import functools

import jax
import jax.numpy as jnp
from jax import lax
from jax.experimental import pallas as pl
from jax.experimental.pallas import tpu as pltpu
from jax.sharding import PartitionSpec as P

BF = jnp.bfloat16
F32 = jnp.float32


def first_slope(value):
    sig = jax.nn.sigmoid(value)
    return sig * (1.0 + value * (1.0 - sig))


def second_slope(value):
    sig = jax.nn.sigmoid(value)
    return sig * (1.0 - sig) * (2.0 + value * (1.0 - 2.0 * sig))


def swap(value, axis, bit):
    return lax.ppermute(value, axis, [(i, i ^ bit) for i in range(lax.axis_size(axis))])


def after(value, *others):
    return lax.optimization_barrier((value,) + others)[0]


def bits_of(size):
    found = []
    bit = 1
    while bit < size:
        found.append(bit)
        bit *= 2
    return found


def onehots(labels, copies):
    copy = labels[1:2, :].astype(F32)
    return [(copy == float(c)).astype(F32) for c in range(copies)]


def times_tokens(core, part, pairs, mine, other, held, rows):
    total = None
    for j in range(pairs):
        for value, side in ((mine, core), (other, 1 - core)):
            columns = pl.ds(pl.multiple_of((2 * j + side) * part, part), part)
            term = lax.dot_general(
                value[:, pl.ds(j * part, part)],
                held[rows, columns],
                (((1,), (1,)), ((), ())),
                preferred_element_type=F32,
            )
            total = term if total is None else total + term
    return total


def contract(core, part, pairs, delta, held, rows, send, keep, before):
    for j in range(pairs):
        place = pl.ds(j * part, part)
        for k, (out, side) in enumerate(((send, 1 - core), (keep, core))):
            columns = pl.ds(pl.multiple_of((2 * j + side) * part, part), part)
            term = jnp.dot(delta, held[rows, columns], preferred_element_type=F32)
            if before is not None:
                term = before[k][:, place] + term
            out[:, place] = term.astype(out.dtype)


def by_copy(delta, hots):
    delta = delta.astype(F32)
    return jnp.concatenate([delta * hot for hot in hots], 0).astype(BF)


def prepare_kernel(wide, side_of, stride, scalars, upstream, value_weight, weight, up, labels, sent, turned):
    me = scalars[0]
    group = 128 // wide
    columns = pl.ds(pl.multiple_of((me // group) * 128, 128), 128)
    turned[...] = value_weight[:, columns].astype(F32).T
    own = pl.ds(pl.multiple_of((me % group) * wide, wide), wide)
    weight[...] = turned[own, :].astype(BF)
    up[...] = upstream[...].astype(F32).T.astype(BF)
    row = lax.broadcasted_iota(jnp.int32, labels.shape, 0)
    both = jnp.where(row == 0, scalars[2], jnp.where(row == 1, scalars[3], 0))
    labels[...] = both.astype(F32).astype(BF)
    every_second(up, 1 - side_of(me), stride, wide, sent)
    sent[pl.ds(up.shape[0] // 2, 16), :] = labels[...]


def every_second(source, side, stride, wide, target, columns=slice(None)):
    for k in range(source.shape[0] // wide // 2):
        place = (2 * (k // stride) + side) * stride + k % stride
        block = pl.ds(pl.multiple_of(place * wide, wide), wide)
        target[pl.ds(k * wide, wide), columns] = source[block, :]


def join_kernel(wide, side_of, stride, next_side, next_stride, scalars, up, labels, came, new_up, new_labels, *sent):
    me = scalars[0]
    half, long = up.shape[0] // 2, up.shape[1]
    every_second(up, side_of(me), stride, wide, new_up, pl.ds(0, long))
    new_up[:, pl.ds(long, long)] = came[pl.ds(0, half), :]
    new_labels[:, pl.ds(0, long)] = labels[...]
    new_labels[:, pl.ds(long, long)] = came[pl.ds(half, 16), :]
    if sent:
        every_second(new_up, 1 - next_side(me), next_stride, wide, sent[0])
        sent[0][pl.ds(half // 2, 16), :] = new_labels[...]


def put_together(pieces, held):
    row = 0
    for piece in pieces:
        held[pl.ds(row, piece.shape[0]), :] = piece[...]
        row += piece.shape[0]


def times_weight(quarter, part, weight, held, rows):
    wide = weight.shape[0] * part // held.shape[1]
    total = None
    for i in range(weight.shape[0] // wide):
        columns = pl.ds(pl.multiple_of((quarter ^ i) * part, part), part)
        term = lax.dot_general(
            weight[pl.ds(i * wide, wide), :],
            held[rows, columns],
            (((1,), (1,)), ((), ())),
            preferred_element_type=F32,
        )
        total = term if total is None else total + term
    return total


def tiles_of(held, body):
    tile = min(held.shape[0], 1024)
    if held.shape[0] == tile:
        body(pl.ds(0, tile), False)
        return

    def step(i, none):
        body(pl.ds(pl.multiple_of(i * tile, tile), tile), True)

    lax.fori_loop(0, held.shape[0] // tile, step, None)


def primal_kernel(part, scalars, *refs):
    pieces, (weight, held, primal) = refs[:-3], refs[-3:]
    put_together(pieces, held)

    def body(rows, _):
        primal[:, rows] = times_weight(scalars[1], part, weight, held, rows)

    tiles_of(held, body)


def first_kernel(sizes, places, scalars, *refs):
    part, pairs, copies, length = sizes
    pieces, refs = refs[:-12], refs[-12:]
    all_up, all_labels, weight, held_early, primal_early, *refs = refs
    held_late, primal_late, up, labels, send, keep, sums = refs
    quarter = scalars[1]
    put_together(pieces, held_late)
    primal_late[...] = times_weight(quarter, part, weight, held_late, pl.ds(0, held_late.shape[0]))
    rows = up.shape[1] // len(places)
    for i, place in enumerate(places):
        up[:, pl.ds(i * rows, rows)] = all_up[:, pl.ds(place * rows, rows)]
        labels[:, pl.ds(i * rows, rows)] = all_labels[:, pl.ds(place * rows, rows)]

    def terms(held, primal, rows, start, send, before):
        lanes = pl.ds(start + rows.start, rows.size)
        hots = onehots(labels[:, lanes], copies)
        forget = labels[0:1, lanes].astype(F32)
        slope = first_slope(primal[:, rows])
        delta = (forget * up[:, lanes].astype(F32) * slope / length).astype(BF)
        contract(quarter % 2, part, pairs, by_copy(delta, hots), held, rows, send, keep, before)

    if held_early.shape[0] > 1024:
        sums[...] = jnp.zeros_like(sums)
        keep[...] = jnp.zeros_like(keep)

    def body(rows, more):
        terms(held_early, primal_early, rows, 0, sums, (sums, keep) if more else None)

    tiles_of(held_early, body)
    every = pl.ds(0, held_late.shape[0])
    terms(held_late, primal_late, every, held_early.shape[0], send, (sums, keep))


def sort_kernel(sizes, rows, scalars, rate, *refs):
    part, pairs, copies, length = sizes
    early, late, (up, labels, own, own_side, sent_side, *refs) = refs[:2], refs[2:4], refs[4:]
    pieces, sent = refs[:-1], refs[-1]
    core = scalars[1] % 2
    wide = up.shape[0]
    counts = [jnp.int32(0), jnp.int32(0)]
    start = 0
    for held, primal in (early, late):
        for i in range(held.shape[0] // rows):
            place = pl.ds(i * rows, rows)
            label = labels[:, pl.ds(start, rows)].astype(F32)
            forget, copy = label[0:1, :], label[1:2, :]
            upward = up[:, pl.ds(start, rows)].astype(F32)
            start += rows
            own_rate = sum((copy == float(c)).astype(F32) * rate[c] for c in range(copies))
            factor = own_rate * (forget * upward * second_slope(primal[:, place]) / length)
            signed = (1.0 - 2.0 * forget) * upward
            mine = (jnp.max(copy).astype(jnp.int32) == core).astype(jnp.int32)
            for k, (tokens, side) in enumerate(((own, own_side), (sent, sent_side))):
                at = pl.ds(pl.multiple_of(counts[k] * rows, rows), rows)
                here = mine if k == 0 else 1 - mine

                @pl.when(here == 1)
                def _(tokens=tokens, side=side, at=at):
                    tokens[at, :] = held[place, :]
                    side[pl.ds(0, wide), at] = signed.astype(BF)
                    side[pl.ds(wide, wide), at] = factor.astype(BF)

                counts[k] = counts[k] + here
    for i, piece in enumerate(pieces):
        piece[...] = sent[pl.ds(i * piece.shape[0], piece.shape[0]), :]


def in_tiles_of(parts, out, body):
    tile = min(parts[0][0].shape[0], 1024)
    if parts[0][0].shape[0] == tile:
        for i, tokens in enumerate(parts):
            body(tokens, pl.ds(0, tile), out, i > 0)
        return
    out[...] = jnp.zeros_like(out)
    for tokens in parts:

        def step(i, none):
            body(tokens, pl.ds(pl.multiple_of(i * tile, tile), tile), out, True)

        lax.fori_loop(0, tokens[0].shape[0] // tile, step, None)


def add_terms(delta, held, rows, out, more):
    term = jnp.dot(delta, held[rows, :], preferred_element_type=F32)
    out[...] = out[...] + term if more else term


def second_kernel(sizes, scalars, *refs):
    part, pairs, copies, length = sizes
    early, pieces, (side, mine, other, held, send, keep) = refs[:2], refs[2:-6], refs[-6:]
    late = (held, side)
    core = scalars[1] % 2
    put_together(pieces, held)

    def body(tokens, rows, keep, more):
        held, side = tokens
        altered = times_tokens(core, part, pairs, mine, other, held, rows)
        upward = side[pl.ds(0, altered.shape[0]), rows].astype(F32)
        delta = (upward * first_slope(altered) / length).astype(BF)
        add_terms(delta, held, rows, keep, more)

    in_tiles_of((early, late), keep, body)
    send[...] = keep[...].astype(BF)


def third_kernel(sizes, scalars, *refs):
    part, pairs, copies, length = sizes
    early, late, (local, summed, came, send, keep, tangent, curv) = refs[:2], refs[2:4], refs[4:]
    core = scalars[1] % 2
    tangent[...] = (summed[...] + came[...].astype(F32)).astype(BF)

    def body(tokens, rows, curv, more):
        held, side = tokens
        forward = lax.dot_general(
            tangent[...], held[rows, :], (((1,), (1,)), ((), ())), preferred_element_type=F32
        )
        wide = forward.shape[0]
        delta = (side[pl.ds(wide, wide), rows].astype(F32) * forward).astype(BF)
        add_terms(delta, held, rows, curv, more)

    in_tiles_of((early, late), curv, body)
    for j in range(pairs):
        for out, side in ((send, 1 - core), (keep, core)):
            columns = pl.ds(pl.multiple_of((2 * j + side) * part, part), part)
            value = local[:, columns] - curv[:, columns]
            out[:, pl.ds(j * part, part)] = value.astype(out.dtype)


def add_kernel(mine, came, total, sent):
    value = mine[...] + came[...].astype(F32)
    total[...] = value
    sent[...] = value.astype(BF)


def attack_kernel(scalars, rate, mine, came, weight, own, sent):
    quarter = scalars[1]
    part = weight.shape[1]
    wide = own.shape[0]
    for j in range(mine.shape[1] // part):
        place = quarter ^ (2 * j + quarter % 2)
        start = weight[pl.ds(pl.multiple_of(place * wide, wide), wide), :].astype(F32)
        columns = pl.ds(j * part, part)
        for out, c in ((own, quarter % 2), (sent, 1 - quarter % 2)):
            rows = pl.ds(pl.multiple_of(c * wide, wide), wide)
            grad = mine[rows, columns] + came[rows, columns].astype(F32)
            out[:, columns] = (start - rate[c] * grad).astype(BF)


def halve_kernel(bit, scalars, mine, came, total, sent, whole):
    whole[...] = mine[...] + came[...].astype(F32)
    half = total.shape[1]
    side = (scalars[1] // bit) % 2
    total[...] = whole[:, pl.ds(pl.multiple_of(side * half, half), half)]
    sent[...] = whole[:, pl.ds(pl.multiple_of((1 - side) * half, half), half)].astype(BF)


def result_kernel(scale, mine, came, result):
    result[...] = (scale * (mine[...] + came[...].astype(F32))).astype(BF)


def place_kernel(order, scalars, *refs):
    blocks, (out, joined) = refs[:-2], refs[-2:]
    me = scalars[0]
    wide = blocks[0].shape[0]
    for r, block in zip(order, blocks):
        joined[pl.ds(pl.multiple_of((me ^ r) * wide, wide), wide), :] = block[...]
    out[...] = joined[...].T.astype(F32)


def run(kernel, scalars, arrays, outs, scratch=()):
    nbytes = sum(a.size * a.dtype.itemsize for a in arrays)
    nbytes += sum(s[0] * s[1] * jnp.dtype(t).itemsize for s, t in outs)
    smem = pl.BlockSpec(memory_space=pltpu.SMEM)
    vmem = pl.BlockSpec(memory_space=pltpu.VMEM)
    return pl.pallas_call(
        kernel,
        out_shape=[jax.ShapeDtypeStruct(s, t) for s, t in outs],
        in_specs=[smem] * len(scalars) + [vmem] * len(arrays),
        out_specs=[vmem] * len(outs),
        scratch_shapes=[pltpu.VMEM(s, t) for s, t in scratch],
        compiler_params=pltpu.CompilerParams(vmem_limit_bytes=nbytes + (8 << 20)),
    )(*scalars, *arrays)


def local(tokens, upstream, value_weight, forget_label, copy_index, adv_rate):
    dp, fsdp = lax.axis_size("dp"), lax.axis_size("fsdp")
    rows, features = tokens.shape
    outs = upstream.shape[1]
    wide = outs // dp
    part = features // fsdp
    pairs = fsdp // 2
    copies = adv_rate.shape[0]
    seq_length = rows * fsdp
    me = lax.axis_index("dp").astype(jnp.int32)
    quarter = lax.axis_index("fsdp").astype(jnp.int32)
    scalars = jnp.stack([me, quarter, forget_label[0], copy_index[0]])
    dp_bits = bits_of(dp)[::-1]
    far_bits = bits_of(fsdp)[1:]
    up_bits = dp_bits[::-1]
    up_bits = up_bits[1:2] + up_bits[:1] + up_bits[2:]
    strides = [2 ** sum(low < bit for low in up_bits[i:]) for i, bit in enumerate(up_bits)]

    def side_of(bit):
        return lambda me: (me // bit) % 2

    weight, up, labels, sent = run(
        functools.partial(prepare_kernel, wide, side_of(up_bits[0]), strides[0]),
        [scalars],
        [upstream, value_weight],
        [((wide, part), BF), ((outs, rows), BF), ((16, rows), BF), ((outs // 2 + 16, rows), BF)],
        [((128, part), F32)],
    )

    half_rows = rows // 2
    first = {0: tokens[:half_rows]}
    second = {0: tokens[half_rows:]}
    near = [swap(tokens, "dp", 1)]
    whole = {1: near[0]}

    def send(value, bit, *others):
        if bit == 1:
            others += (near[max(len(near) - 2, 0)],)
        if others:
            value = after(value, *others)
        came = swap(value, "dp", bit)
        if bit == 1:
            near.append(came)
        return came

    ties = ()
    top_bit = dp_bits[0]
    for step, up_bit in enumerate(up_bits, 1):
        if step == len(dp_bits) and step > 1:
            sent = after(sent, first[top_bit | up_bits[0]])
        came_up = swap(sent, "dp", up_bit)
        ready = [r for r in range(2, dp) if bin(r).count("1") == step]
        firsts, seconds = {}, {}
        for r in ready:
            bit = r & -r
            way = 2 * bit if r == dp - 1 and dp > 2 else bit
            firsts[r] = send(first[r ^ way], way, *(ties if way == 1 else ()))
        for r in ready:
            bit = r & -r
            others = (firsts[r],) if step == 1 else (came_up,) if step == 2 and bit == 1 else ()
            seconds[r] = send(second[r ^ bit], bit, *others)
        first.update(firsts)
        second.update(seconds)
        ties = (came_up,) if step == 1 else ()
        high, long = up.shape[0] // 2, 2 * up.shape[1]
        shapes = [((high, long), BF), ((16, long), BF)]
        if step < len(dp_bits):
            shapes.append(((high // 2 + 16, long), BF))
        following = (side_of(up_bits[step]), strides[step]) if step < len(dp_bits) else (None, None)
        joined = run(
            functools.partial(join_kernel, wide, side_of(up_bit), strides[step - 1], *following),
            [scalars],
            [up, labels, came_up],
            shapes,
        )
        up, labels = joined[:2]
        sent = joined[-1]
    order = [0]
    for bit in up_bits:
        order = order + [r ^ bit for r in order]
    late = [r for r in range(dp) if r & dp_bits[0] and r & 1]
    early = [r for r in range(dp) if r not in late]

    def pieces_of(blocks):
        return [x for r in blocks for x in ([whole[r]] if r in whole else [first[r], second[r]])]

    weight = after(weight, first[dp_bits[0]])
    for bit in bits_of(fsdp):
        weight = jnp.concatenate([weight, swap(weight, "fsdp", bit)])

    def total(keep, came, bits):
        for bit in bits:
            keep, sent = run(add_kernel, [], [keep, came], [(keep.shape, F32), (keep.shape, BF)])
            came = swap(sent, "fsdp", bit)
        return keep, came

    sizes = (part, pairs, copies, seq_length)
    stacked = (copies * wide, features // 2)
    count = rows * len(early)
    held_early, primal_early = run(
        functools.partial(primal_kernel, part),
        [scalars],
        pieces_of(early) + [weight],
        [((count, features), BF), ((wide, count), F32)],
    )
    count = rows * len(late)
    held_late, primal_late, up, labels, send, keep = run(
        functools.partial(first_kernel, sizes, [order.index(r) for r in early + late]),
        [scalars],
        pieces_of(late) + [up, labels, weight, held_early, primal_early],
        [
            ((count, features), BF),
            ((wide, count), F32),
            ((wide, dp * rows), BF),
            ((16, dp * rows), BF),
            (stacked, BF),
            (stacked, F32),
        ],
        [(stacked, F32)],
    )
    summed, came = total(keep, swap(send, "fsdp", 1), far_bits)
    labels = after(labels, summed)
    taken = ((dp // 2 * rows, features), BF)
    beside = ((2 * wide, dp // 2 * rows), BF)
    cut = ((half_rows, features), BF)
    own, own_side, sent_side, *sent = run(
        functools.partial(sort_kernel, sizes, rows),
        [scalars, adv_rate],
        [held_early, primal_early, held_late, primal_late, up, labels],
        [taken, beside, beside] + [cut] * dp,
        [taken],
    )
    came_side = swap(sent_side, "fsdp", 1)
    came_pieces = [swap(piece, "fsdp", 1) for piece in sent]
    half, full = (wide, features // 2), (wide, features)
    attacked, sent = run(
        attack_kernel, [scalars, adv_rate], [summed, came, weight], [(half, BF), (half, BF)]
    )
    held, send, keep = run(
        functools.partial(second_kernel, sizes),
        [scalars],
        [own, own_side, *came_pieces, came_side, attacked, swap(sent, "fsdp", 1)],
        [taken, (full, BF), (full, F32)],
    )
    mine = [own, own_side, held, came_side]
    send, keep = run(
        functools.partial(third_kernel, sizes),
        [scalars],
        [*mine, keep, *total(keep, swap(send, "fsdp", far_bits[0]), far_bits[1:])],
        [(half, BF), (half, F32)],
        [(full, BF), (full, F32)],
    )

    came = swap(send, "fsdp", 1)
    for bit in far_bits[::-1]:
        shape = (wide, keep.shape[1] // 2)
        keep, sent = run(
            functools.partial(halve_kernel, bit),
            [scalars],
            [keep, came],
            [(shape, F32), (shape, BF)],
            [(keep.shape, F32)],
        )
        came = swap(sent, "fsdp", bit)
    scale = (float(seq_length) / float(dp)) ** 0.5
    (result,) = run(
        functools.partial(result_kernel, scale), [], [keep, came], [((wide, part), BF)]
    )
    upper = [i ^ (i >> 1) for i in range(dp // 2)][::-1]
    came_order = [0] + [2 * i for i in upper if i] + [2 * i + 1 for i in upper]
    blocks = [swap(result, "dp", r) if r else result for r in came_order]
    (placed,) = run(
        functools.partial(place_kernel, came_order),
        [scalars],
        blocks,
        [((part, outs), F32)],
        [((outs, part), BF)],
    )
    return placed


def solution(mesh):
    in_specs = (
        P(("dp", "fsdp"), None),
        P(("dp", "fsdp"), None),
        P("fsdp", None),
        P("dp"),
        P("dp"),
        P(),
    )
    out_specs = P("fsdp", None)
    return jax.shard_map(local, mesh=mesh, in_specs=in_specs, out_specs=out_specs, check_vma=False)
```

```python
import functools

import jax
import jax.numpy as jnp
from jax import lax
from jax.experimental import pallas as pl
from jax.experimental.pallas import tpu as pltpu
from jax.sharding import PartitionSpec as P

BF = jnp.bfloat16
F32 = jnp.float32


def first_slope(value):
    sig = jax.nn.sigmoid(value)
    return sig * (1.0 + value * (1.0 - sig))


def second_slope(value):
    sig = jax.nn.sigmoid(value)
    return sig * (1.0 - sig) * (2.0 + value * (1.0 - 2.0 * sig))


def swap(value, axis, bit):
    return lax.ppermute(value, axis, [(i, i ^ bit) for i in range(lax.axis_size(axis))])


def after(value, *others):
    return lax.optimization_barrier((value,) + others)[0]


def bits_of(size):
    found = []
    bit = 1
    while bit < size:
        found.append(bit)
        bit *= 2
    return found


def onehots(labels, copies):
    copy = labels[1:2, :].astype(F32)
    return [(copy == float(c)).astype(F32) for c in range(copies)]


def times_tokens(core, part, pairs, mine, other, held, rows):
    total = None
    for j in range(pairs):
        for value, side in ((mine, core), (other, 1 - core)):
            columns = pl.ds(pl.multiple_of((2 * j + side) * part, part), part)
            term = lax.dot_general(
                value[:, pl.ds(j * part, part)],
                held[rows, columns],
                (((1,), (1,)), ((), ())),
                preferred_element_type=F32,
            )
            total = term if total is None else total + term
    return total


def contract(core, part, pairs, delta, held, rows, send, keep, before):
    for j in range(pairs):
        place = pl.ds(j * part, part)
        for k, (out, side) in enumerate(((send, 1 - core), (keep, core))):
            columns = pl.ds(pl.multiple_of((2 * j + side) * part, part), part)
            term = jnp.dot(delta, held[rows, columns], preferred_element_type=F32)
            if before is not None:
                term = before[k][:, place] + term
            out[:, place] = term.astype(out.dtype)


def by_copy(delta, hots):
    delta = delta.astype(F32)
    return jnp.concatenate([delta * hot for hot in hots], 0).astype(BF)


def prepare_kernel(wide, side_of, stride, scalars, upstream, value_weight, weight, up, labels, sent, turned):
    me = scalars[0]
    group = 128 // wide
    columns = pl.ds(pl.multiple_of((me // group) * 128, 128), 128)
    turned[...] = value_weight[:, columns].astype(F32).T
    own = pl.ds(pl.multiple_of((me % group) * wide, wide), wide)
    weight[...] = turned[own, :].astype(BF)
    up[...] = upstream[...].astype(F32).T.astype(BF)
    row = lax.broadcasted_iota(jnp.int32, labels.shape, 0)
    both = jnp.where(row == 0, scalars[2], jnp.where(row == 1, scalars[3], 0))
    labels[...] = both.astype(F32).astype(BF)
    every_second(up, 1 - side_of(me), stride, wide, sent)
    sent[pl.ds(up.shape[0] // 2, 16), :] = labels[...]


def every_second(source, side, stride, wide, target, columns=slice(None)):
    for k in range(source.shape[0] // wide // 2):
        place = (2 * (k // stride) + side) * stride + k % stride
        block = pl.ds(pl.multiple_of(place * wide, wide), wide)
        target[pl.ds(k * wide, wide), columns] = source[block, :]


def join_kernel(wide, side_of, stride, next_side, next_stride, scalars, up, labels, came, new_up, new_labels, *sent):
    me = scalars[0]
    half, long = up.shape[0] // 2, up.shape[1]
    every_second(up, side_of(me), stride, wide, new_up, pl.ds(0, long))
    new_up[:, pl.ds(long, long)] = came[pl.ds(0, half), :]
    new_labels[:, pl.ds(0, long)] = labels[...]
    new_labels[:, pl.ds(long, long)] = came[pl.ds(half, 16), :]
    if sent:
        every_second(new_up, 1 - next_side(me), next_stride, wide, sent[0])
        sent[0][pl.ds(half // 2, 16), :] = new_labels[...]


def put_together(pieces, held):
    row = 0
    for piece in pieces:
        held[pl.ds(row, piece.shape[0]), :] = piece[...]
        row += piece.shape[0]


def times_weight(quarter, part, weight, held, rows):
    wide = weight.shape[0] * part // held.shape[1]
    total = None
    for i in range(weight.shape[0] // wide):
        columns = pl.ds(pl.multiple_of((quarter ^ i) * part, part), part)
        term = lax.dot_general(
            weight[pl.ds(i * wide, wide), :],
            held[rows, columns],
            (((1,), (1,)), ((), ())),
            preferred_element_type=F32,
        )
        total = term if total is None else total + term
    return total


def tiles_of(held, body):
    tile = min(held.shape[0], 1024)
    if held.shape[0] == tile:
        body(pl.ds(0, tile), False)
        return

    def step(i, none):
        body(pl.ds(pl.multiple_of(i * tile, tile), tile), True)

    lax.fori_loop(0, held.shape[0] // tile, step, None)


def primal_kernel(part, scalars, *refs):
    pieces, (weight, held, primal) = refs[:-3], refs[-3:]
    put_together(pieces, held)

    def body(rows, _):
        primal[:, rows] = times_weight(scalars[1], part, weight, held, rows)

    tiles_of(held, body)


def first_kernel(sizes, places, scalars, *refs):
    part, pairs, copies, length = sizes
    pieces, refs = refs[:-12], refs[-12:]
    all_up, all_labels, weight, held_early, primal_early, *refs = refs
    held_late, primal_late, up, labels, send, keep, sums = refs
    quarter = scalars[1]
    put_together(pieces, held_late)
    primal_late[...] = times_weight(quarter, part, weight, held_late, pl.ds(0, held_late.shape[0]))
    rows = up.shape[1] // len(places)
    for i, place in enumerate(places):
        up[:, pl.ds(i * rows, rows)] = all_up[:, pl.ds(place * rows, rows)]
        labels[:, pl.ds(i * rows, rows)] = all_labels[:, pl.ds(place * rows, rows)]

    def terms(held, primal, rows, start, send, before):
        lanes = pl.ds(start + rows.start, rows.size)
        hots = onehots(labels[:, lanes], copies)
        forget = labels[0:1, lanes].astype(F32)
        slope = first_slope(primal[:, rows])
        delta = (forget * up[:, lanes].astype(F32) * slope / length).astype(BF)
        contract(quarter % 2, part, pairs, by_copy(delta, hots), held, rows, send, keep, before)

    if held_early.shape[0] > 1024:
        sums[...] = jnp.zeros_like(sums)
        keep[...] = jnp.zeros_like(keep)

    def body(rows, more):
        terms(held_early, primal_early, rows, 0, sums, (sums, keep) if more else None)

    tiles_of(held_early, body)
    every = pl.ds(0, held_late.shape[0])
    terms(held_late, primal_late, every, held_early.shape[0], send, (sums, keep))


def sort_kernel(sizes, rows, scalars, rate, *refs):
    part, pairs, copies, length = sizes
    early, late, (up, labels, own, own_side, sent_side, *refs) = refs[:2], refs[2:4], refs[4:]
    pieces, sent = refs[:-1], refs[-1]
    core = scalars[1] % 2
    wide = up.shape[0]
    counts = [jnp.int32(0), jnp.int32(0)]
    start = 0
    for held, primal in (early, late):
        for i in range(held.shape[0] // rows):
            place = pl.ds(i * rows, rows)
            label = labels[:, pl.ds(start, rows)].astype(F32)
            forget, copy = label[0:1, :], label[1:2, :]
            upward = up[:, pl.ds(start, rows)].astype(F32)
            start += rows
            own_rate = sum((copy == float(c)).astype(F32) * rate[c] for c in range(copies))
            factor = own_rate * (forget * upward * second_slope(primal[:, place]) / length)
            signed = (1.0 - 2.0 * forget) * upward
            mine = (jnp.max(copy).astype(jnp.int32) == core).astype(jnp.int32)
            for k, (tokens, side) in enumerate(((own, own_side), (sent, sent_side))):
                at = pl.ds(pl.multiple_of(counts[k] * rows, rows), rows)
                here = mine if k == 0 else 1 - mine

                @pl.when(here == 1)
                def _(tokens=tokens, side=side, at=at):
                    tokens[at, :] = held[place, :]
                    side[pl.ds(0, wide), at] = signed.astype(BF)
                    side[pl.ds(wide, wide), at] = factor.astype(BF)

                counts[k] = counts[k] + here
    for i, piece in enumerate(pieces):
        piece[...] = sent[pl.ds(i * piece.shape[0], piece.shape[0]), :]


def in_tiles_of(parts, out, body):
    tile = min(parts[0][0].shape[0], 1024)
    if parts[0][0].shape[0] == tile:
        for i, tokens in enumerate(parts):
            body(tokens, pl.ds(0, tile), out, i > 0)
        return
    out[...] = jnp.zeros_like(out)
    for tokens in parts:

        def step(i, none):
            body(tokens, pl.ds(pl.multiple_of(i * tile, tile), tile), out, True)

        lax.fori_loop(0, tokens[0].shape[0] // tile, step, None)


def add_terms(delta, held, rows, out, more):
    term = jnp.dot(delta, held[rows, :], preferred_element_type=F32)
    out[...] = out[...] + term if more else term


def second_kernel(sizes, scalars, *refs):
    part, pairs, copies, length = sizes
    early, pieces, (side, mine, other, held, send, keep) = refs[:2], refs[2:-6], refs[-6:]
    late = (held, side)
    core = scalars[1] % 2
    put_together(pieces, held)

    def body(tokens, rows, keep, more):
        held, side = tokens
        altered = times_tokens(core, part, pairs, mine, other, held, rows)
        upward = side[pl.ds(0, altered.shape[0]), rows].astype(F32)
        delta = (upward * first_slope(altered) / length).astype(BF)
        add_terms(delta, held, rows, keep, more)

    in_tiles_of((early, late), keep, body)
    send[...] = keep[...].astype(BF)


def third_kernel(sizes, scalars, *refs):
    part, pairs, copies, length = sizes
    early, late, (local, summed, came, send, keep, tangent, curv) = refs[:2], refs[2:4], refs[4:]
    core = scalars[1] % 2
    tangent[...] = (summed[...] + came[...].astype(F32)).astype(BF)

    def body(tokens, rows, curv, more):
        held, side = tokens
        forward = lax.dot_general(
            tangent[...], held[rows, :], (((1,), (1,)), ((), ())), preferred_element_type=F32
        )
        wide = forward.shape[0]
        delta = (side[pl.ds(wide, wide), rows].astype(F32) * forward).astype(BF)
        add_terms(delta, held, rows, curv, more)

    in_tiles_of((early, late), curv, body)
    for j in range(pairs):
        for out, side in ((send, 1 - core), (keep, core)):
            columns = pl.ds(pl.multiple_of((2 * j + side) * part, part), part)
            value = local[:, columns] - curv[:, columns]
            out[:, pl.ds(j * part, part)] = value.astype(out.dtype)


def add_kernel(mine, came, total, sent):
    value = mine[...] + came[...].astype(F32)
    total[...] = value
    sent[...] = value.astype(BF)


def attack_kernel(scalars, rate, mine, came, weight, own, sent):
    quarter = scalars[1]
    part = weight.shape[1]
    wide = own.shape[0]
    for j in range(mine.shape[1] // part):
        place = quarter ^ (2 * j + quarter % 2)
        start = weight[pl.ds(pl.multiple_of(place * wide, wide), wide), :].astype(F32)
        columns = pl.ds(j * part, part)
        for out, c in ((own, quarter % 2), (sent, 1 - quarter % 2)):
            rows = pl.ds(pl.multiple_of(c * wide, wide), wide)
            grad = mine[rows, columns] + came[rows, columns].astype(F32)
            out[:, columns] = (start - rate[c] * grad).astype(BF)


def halve_kernel(bit, scalars, mine, came, total, sent, whole):
    whole[...] = mine[...] + came[...].astype(F32)
    half = total.shape[1]
    side = (scalars[1] // bit) % 2
    total[...] = whole[:, pl.ds(pl.multiple_of(side * half, half), half)]
    sent[...] = whole[:, pl.ds(pl.multiple_of((1 - side) * half, half), half)].astype(BF)


def result_kernel(scale, mine, came, result):
    result[...] = (scale * (mine[...] + came[...].astype(F32))).astype(BF)


def place_kernel(order, scalars, *refs):
    blocks, (out, joined) = refs[:-2], refs[-2:]
    me = scalars[0]
    wide = blocks[0].shape[0]
    for r, block in zip(order, blocks):
        joined[pl.ds(pl.multiple_of((me ^ r) * wide, wide), wide), :] = block[...]
    out[...] = joined[...].T.astype(F32)


def run(kernel, scalars, arrays, outs, scratch=()):
    nbytes = sum(a.size * a.dtype.itemsize for a in arrays)
    nbytes += sum(s[0] * s[1] * jnp.dtype(t).itemsize for s, t in outs)
    smem = pl.BlockSpec(memory_space=pltpu.SMEM)
    vmem = pl.BlockSpec(memory_space=pltpu.VMEM)
    return pl.pallas_call(
        kernel,
        out_shape=[jax.ShapeDtypeStruct(s, t) for s, t in outs],
        in_specs=[smem] * len(scalars) + [vmem] * len(arrays),
        out_specs=[vmem] * len(outs),
        scratch_shapes=[pltpu.VMEM(s, t) for s, t in scratch],
        compiler_params=pltpu.CompilerParams(vmem_limit_bytes=nbytes + (8 << 20)),
    )(*scalars, *arrays)


def local(tokens, upstream, value_weight, forget_label, copy_index, adv_rate):
    dp, fsdp = lax.axis_size("dp"), lax.axis_size("fsdp")
    rows, features = tokens.shape
    outs = upstream.shape[1]
    wide = outs // dp
    part = features // fsdp
    pairs = fsdp // 2
    copies = adv_rate.shape[0]
    seq_length = rows * fsdp
    me = lax.axis_index("dp").astype(jnp.int32)
    quarter = lax.axis_index("fsdp").astype(jnp.int32)
    scalars = jnp.stack([me, quarter, forget_label[0], copy_index[0]])
    dp_bits = bits_of(dp)[::-1]
    far_bits = bits_of(fsdp)[1:]
    up_bits = dp_bits[::-1]
    up_bits = up_bits[1:2] + up_bits[:1] + up_bits[2:]
    strides = [2 ** sum(low < bit for low in up_bits[i:]) for i, bit in enumerate(up_bits)]

    def side_of(bit):
        return lambda me: (me // bit) % 2

    weight, up, labels, sent = run(
        functools.partial(prepare_kernel, wide, side_of(up_bits[0]), strides[0]),
        [scalars],
        [upstream, value_weight],
        [((wide, part), BF), ((outs, rows), BF), ((16, rows), BF), ((outs // 2 + 16, rows), BF)],
        [((128, part), F32)],
    )

    half_rows = rows // 2
    first = {0: tokens[:half_rows]}
    second = {0: tokens[half_rows:]}
    near = [swap(tokens, "dp", 1)]
    whole = {1: near[0]}

    def send(value, bit, *others):
        if bit == 1:
            others += (near[max(len(near) - 2, 0)],)
        if others:
            value = after(value, *others)
        came = swap(value, "dp", bit)
        if bit == 1:
            near.append(came)
        return came

    ties = ()
    top_bit = dp_bits[0]
    for step, up_bit in enumerate(up_bits, 1):
        if step == len(dp_bits) and step > 1:
            sent = after(sent, first[top_bit | up_bits[0]])
        came_up = swap(sent, "dp", up_bit)
        ready = [r for r in range(2, dp) if bin(r).count("1") == step]
        firsts, seconds = {}, {}
        for r in ready:
            bit = r & -r
            way = 2 * bit if r == dp - 1 and dp > 2 else bit
            firsts[r] = send(first[r ^ way], way, *(ties if way == 1 else ()))
        for r in ready:
            bit = r & -r
            others = (firsts[r],) if step == 1 else (came_up,) if step == 2 and bit == 1 else ()
            seconds[r] = send(second[r ^ bit], bit, *others)
        first.update(firsts)
        second.update(seconds)
        ties = (came_up,) if step == 1 else ()
        high, long = up.shape[0] // 2, 2 * up.shape[1]
        shapes = [((high, long), BF), ((16, long), BF)]
        if step < len(dp_bits):
            shapes.append(((high // 2 + 16, long), BF))
        following = (side_of(up_bits[step]), strides[step]) if step < len(dp_bits) else (None, None)
        joined = run(
            functools.partial(join_kernel, wide, side_of(up_bit), strides[step - 1], *following),
            [scalars],
            [up, labels, came_up],
            shapes,
        )
        up, labels = joined[:2]
        sent = joined[-1]
    order = [0]
    for bit in up_bits:
        order = order + [r ^ bit for r in order]
    late = [r for r in range(dp) if r & dp_bits[0] and r & 1]
    early = [r for r in range(dp) if r not in late]

    def pieces_of(blocks):
        return [x for r in blocks for x in ([whole[r]] if r in whole else [first[r], second[r]])]

    weight = after(weight, first[dp_bits[0]])
    for bit in bits_of(fsdp):
        weight = jnp.concatenate([weight, swap(weight, "fsdp", bit)])

    def total(keep, came, bits):
        for bit in bits:
            keep, sent = run(add_kernel, [], [keep, came], [(keep.shape, F32), (keep.shape, BF)])
            came = swap(sent, "fsdp", bit)
        return keep, came

    sizes = (part, pairs, copies, seq_length)
    stacked = (copies * wide, features // 2)
    count = rows * len(early)
    held_early, primal_early = run(
        functools.partial(primal_kernel, part),
        [scalars],
        pieces_of(early) + [weight],
        [((count, features), BF), ((wide, count), F32)],
    )
    count = rows * len(late)
    held_late, primal_late, up, labels, send, keep = run(
        functools.partial(first_kernel, sizes, [order.index(r) for r in early + late]),
        [scalars],
        pieces_of(late) + [up, labels, weight, held_early, primal_early],
        [
            ((count, features), BF),
            ((wide, count), F32),
            ((wide, dp * rows), BF),
            ((16, dp * rows), BF),
            (stacked, BF),
            (stacked, F32),
        ],
        [(stacked, F32)],
    )
    summed, came = total(keep, swap(send, "fsdp", 1), far_bits)
    labels = after(labels, summed)
    taken = ((dp // 2 * rows, features), BF)
    beside = ((2 * wide, dp // 2 * rows), BF)
    cut = ((rows, features), BF)
    own, own_side, sent_side, *sent = run(
        functools.partial(sort_kernel, sizes, rows),
        [scalars, adv_rate],
        [held_early, primal_early, held_late, primal_late, up, labels],
        [taken, beside, beside] + [cut] * (dp // 2),
        [taken],
    )
    came_side = swap(sent_side, "fsdp", 1)
    came_pieces = [swap(piece, "fsdp", 1) for piece in sent]
    half, full = (wide, features // 2), (wide, features)
    attacked, sent = run(
        attack_kernel, [scalars, adv_rate], [summed, came, weight], [(half, BF), (half, BF)]
    )
    held, send, keep = run(
        functools.partial(second_kernel, sizes),
        [scalars],
        [own, own_side, *came_pieces, came_side, attacked, swap(sent, "fsdp", 1)],
        [taken, (full, BF), (full, F32)],
    )
    mine = [own, own_side, held, came_side]
    send, keep = run(
        functools.partial(third_kernel, sizes),
        [scalars],
        [*mine, keep, *total(keep, swap(send, "fsdp", far_bits[0]), far_bits[1:])],
        [(half, BF), (half, F32)],
        [(full, BF), (full, F32)],
    )

    came = swap(send, "fsdp", 1)
    for bit in far_bits[::-1]:
        shape = (wide, keep.shape[1] // 2)
        keep, sent = run(
            functools.partial(halve_kernel, bit),
            [scalars],
            [keep, came],
            [(shape, F32), (shape, BF)],
            [(keep.shape, F32)],
        )
        came = swap(sent, "fsdp", bit)
    scale = (float(seq_length) / float(dp)) ** 0.5
    (result,) = run(
        functools.partial(result_kernel, scale), [], [keep, came], [((wide, part), BF)]
    )
    upper = [i ^ (i >> 1) for i in range(dp // 2)][::-1]
    came_order = [0] + [2 * i for i in upper if i] + [2 * i + 1 for i in upper]
    blocks = [swap(result, "dp", r) if r else result for r in came_order]
    (placed,) = run(
        functools.partial(place_kernel, came_order),
        [scalars],
        blocks,
        [((part, outs), F32)],
        [((outs, part), BF)],
    )
    return placed


def solution(mesh):
    in_specs = (
        P(("dp", "fsdp"), None),
        P(("dp", "fsdp"), None),
        P("fsdp", None),
        P("dp"),
        P("dp"),
        P(),
    )
    out_specs = P("fsdp", None)
    return jax.shard_map(local, mesh=mesh, in_specs=in_specs, out_specs=out_specs, check_vma=False)
```
